32 devices in a mesh: dp: 8 (over z, x), rows: 4 (over y, core).
Axes of the slice: x: 2, y: 2, z: 4, core: 2. Of those that a mesh axis runs over, the one named last changes fastest.
Arguments:
- older_output: bfloat16 [1920, 12, 2048], P(('dp', 'rows')), parts along dimension 0, may hold values from -6 to 6
- newer_output: bfloat16 [1920, 12, 2048], P(('dp', 'rows')), parts along dimension 0, may hold values from -6 to 6
- output_grad: bfloat16 [1920, 12, 2048], P(('dp', 'rows')), parts along dimension 0, may hold values from -6 to 6
- older_weight: bfloat16 [2048, 512], P('rows'), may hold values from -0.1875 to 0.1875
- newer_weight: bfloat16 [2048, 512], P('rows'), may hold values from -0.1875 to 0.1875
- square_point: bfloat16 [512, 512], P('rows'), may hold values from -0.25 to 0.25
- column_point: bfloat16 [512, 512], P('rows'), may hold values from -0.25 to 0.25
- square_kernel: float32 [3, 3, 512], replicated, may hold values from -2.4 to 2.4
- column_kernel: float32 [7, 512], replicated, may hold values from -2.4 to 2.4
Outputs:
- cell_output: bfloat16 [1920, 12, 2048], P(('dp', 'rows')), parts along dimension 0
- older_grad: bfloat16 [1920, 12, 2048], P(('dp', 'rows')), parts along dimension 0
- newer_grad: bfloat16 [1920, 12, 2048], P(('dp', 'rows')), parts along dimension 0
The draws below stay inside these ranges and needn't reach their ends.
There are 8 independent parts, one for each index of `dp`. The reference program is written for one: setup_inputs(seed, part) draws one part's arguments, and reference() takes and returns one part's arrays. A program takes and returns all parts, laid end to end along the dimension named above; an argument that names none is the same for every part. Nothing has to cross between parts.
All inputs are finite; a program needn't handle non-finite values.
Results may differ from the reference program's by a relative error of at most 0.0057.
Values may be sent and summed in bfloat16 or wider, within the bound.
A program may use at most 128 MiB of HBM per device.

```python
import jax
import jax.numpy as jnp

C = 512
CIN = 2048
IMGS = 8
HEIGHT = 30
WIDE = 12
OUTC = 2048


def steps_of(own_key, shape, cuts, least, largest):
    def one(dim, blocks):
        heights = jax.random.uniform(jax.random.fold_in(jax.random.fold_in(own_key, 6), dim), (blocks,), jnp.float32, least / len(cuts), largest / len(cuts))
        return jnp.repeat(jnp.exp(heights), shape[dim] // blocks).reshape((-1,) + (1,) * (len(shape) - dim - 1))

    loudness = one(*cuts[0])
    for cut in cuts[1:]:
        loudness = loudness * one(*cut)
    return loudness


def normal_values(key, extent, deviation, bound, pieces=(), kind=jnp.bfloat16):
    factor_of = steps_of(key, extent, pieces, -0.22, 0.18) if pieces else 1.0
    drawn = jax.random.normal(key, extent, jnp.float32) * deviation * factor_of
    return jnp.minimum(jnp.maximum(drawn, -bound), bound).astype(kind)


def setup_inputs(seed: int = 0, part: int = 0) -> dict:
    splits = jax.random.split(jax.random.key(seed), 10)
    part_keys = jax.random.split(jax.random.fold_in(splits[9], part), 10)
    return {
        "older_output": normal_values(part_keys[0], (IMGS * HEIGHT, WIDE, CIN), 1.0, 6.0, ((0, 4),)),
        "newer_output": normal_values(part_keys[1], (IMGS * HEIGHT, WIDE, CIN), 1.0, 6.0, ((0, 4),)),
        "output_grad": normal_values(part_keys[2], (IMGS * HEIGHT, WIDE, OUTC), 1.0, 6.0, ((0, 4),)),
        "older_weight": normal_values(splits[3], (CIN, C), (CIN // 2) ** -0.5, 0.1875, ((0, 4),)),
        "newer_weight": normal_values(splits[4], (CIN, C), (CIN // 2) ** -0.5, 0.1875, ((0, 4),)),
        "square_point": normal_values(splits[5], (C, C), C ** -0.5, 0.25, ((0, 4),)),
        "column_point": normal_values(splits[6], (C, C), C ** -0.5, 0.25, ((0, 4),)),
        "square_kernel": normal_values(splits[7], (3, 3, C), 0.4, 2.4, (), jnp.float32),
        "column_kernel": normal_values(splits[8], (7, C), 0.4, 2.4, (), jnp.float32),
    }


def rows_pad(field, width):
    return jnp.pad(field, ((0, 0), (width, width), (0, 0), (0, 0)))


def square_taps(padded, kernel, flip):
    full = jnp.pad(padded, ((0, 0), (0, 0), (1, 1), (0, 0))).astype(jnp.float32)
    height = full.shape[1] - 2
    across = full.shape[2] - 2
    total = jnp.zeros((full.shape[0], height, across, full.shape[3]), jnp.float32)
    for i in range(3):
        for j in range(3):
            first = 2 - i if flip else i
            second = 2 - j if flip else j
            total = total + full[:, first:first + height, second:second + across, :] * kernel[i, j]
    return total


def column_taps(padded, kernel, flip):
    full = padded.astype(jnp.float32)
    height = full.shape[1] - 6
    total = jnp.zeros((full.shape[0], height, full.shape[2], full.shape[3]), jnp.float32)
    for i in range(7):
        first = 6 - i if flip else i
        total = total + full[:, first:first + height, :, :] * kernel[i]
    return total


def reference(older_output, newer_output, output_grad, older_weight, newer_weight, square_point, column_point, square_kernel, column_kernel):
    stacked, across, channels = older_output.shape
    images = IMGS
    height = HEIGHT
    filters = square_point.shape[0]
    shape_four = (images, height, across, filters)
    pool_kernel = jnp.full((3, 3, filters), 1.0 / 9.0, jnp.float32)
    older_flat = older_output.reshape(-1, channels)
    newer_flat = newer_output.reshape(-1, channels)
    older_mixed = jnp.dot(jnp.maximum(older_flat, 0), older_weight, preferred_element_type=jnp.float32).astype(jnp.bfloat16).reshape(shape_four)
    newer_mixed = jnp.dot(jnp.maximum(newer_flat, 0), newer_weight, preferred_element_type=jnp.float32).astype(jnp.bfloat16).reshape(shape_four)
    square_pre = square_taps(rows_pad(newer_mixed, 1), square_kernel, False).astype(jnp.bfloat16).reshape(-1, filters)
    column_pre = column_taps(rows_pad(older_mixed, 3), column_kernel, False).astype(jnp.bfloat16).reshape(-1, filters)
    pooled = square_taps(rows_pad(older_mixed, 1), pool_kernel, False).reshape(-1, filters)
    square_branch = jnp.dot(square_pre, square_point, preferred_element_type=jnp.float32)
    column_branch = jnp.dot(column_pre, column_point, preferred_element_type=jnp.float32)
    cell_output = jnp.concatenate([square_branch, column_branch, pooled, newer_mixed.reshape(-1, filters).astype(jnp.float32)], axis=1)
    cell_output = cell_output.astype(jnp.bfloat16).reshape(stacked, across, 4 * filters)
    grads = output_grad.reshape(-1, 4 * filters)
    grad_square = grads[:, :filters]
    grad_column = grads[:, filters:2 * filters]
    grad_pool = grads[:, 2 * filters:3 * filters].reshape(shape_four)
    grad_same = grads[:, 3 * filters:].reshape(shape_four)
    square_back = jnp.dot(grad_square, square_point.T, preferred_element_type=jnp.float32).astype(jnp.bfloat16).reshape(shape_four)
    column_back = jnp.dot(grad_column, column_point.T, preferred_element_type=jnp.float32).astype(jnp.bfloat16).reshape(shape_four)
    newer_back = (square_taps(rows_pad(square_back, 1), square_kernel, True) + grad_same.astype(jnp.float32)).astype(jnp.bfloat16)
    older_back = (column_taps(rows_pad(column_back, 3), column_kernel, True) + square_taps(rows_pad(grad_pool, 1), pool_kernel, True)).astype(jnp.bfloat16)
    older_mask = jnp.where(older_flat > 0, 1.0, 0.0).astype(jnp.float32)
    newer_mask = jnp.where(newer_flat > 0, 1.0, 0.0).astype(jnp.float32)
    older_grad = (jnp.dot(older_back.reshape(-1, filters), older_weight.T, preferred_element_type=jnp.float32) * older_mask).astype(jnp.bfloat16)
    newer_grad = (jnp.dot(newer_back.reshape(-1, filters), newer_weight.T, preferred_element_type=jnp.float32) * newer_mask).astype(jnp.bfloat16)
    return cell_output, older_grad.reshape(older_output.shape), newer_grad.reshape(newer_output.shape)
```

```python
import functools

import jax
import jax.numpy as jnp
from jax import lax
from jax.experimental import pallas as pl
from jax.experimental.pallas import tpu as pltpu
from jax.sharding import PartitionSpec as P

MESH = pl.DeviceIdType.MESH
F32 = jnp.float32
BF16 = jnp.bfloat16
LANES = 128

HEIGHT = 30


def with_halo(block, sides, width):
    for axis, dim in sides:
        count = lax.axis_size(axis)
        forward = [(i, i + 1) for i in range(count - 1)]
        backward = [(target, source) for source, target in forward]
        low = lax.ppermute(
            lax.slice_in_dim(block, block.shape[dim] - width, None, axis=dim), axis, forward
        )
        high = lax.ppermute(lax.slice_in_dim(block, 0, width, axis=dim), axis, backward)
        block = jnp.concatenate([low, block, high], axis=dim)
    return block


def same_image(first_row, local_rows, offset):
    row_ids = jnp.arange(local_rows, dtype=jnp.int32) + first_row
    inside = jnp.floor_divide(row_ids + offset, HEIGHT) == jnp.floor_divide(row_ids, HEIGHT)
    return jnp.where(inside, 1.0, 0.0).astype(jnp.float32)[:, None, None]


def square_taps(padded, kernel, flip, first_row):
    full = jnp.pad(padded, ((0, 0), (1, 1), (0, 0))).astype(jnp.float32)
    height = full.shape[0] - 2
    across = full.shape[1] - 2
    total = jnp.zeros((height, across, full.shape[2]), jnp.float32)
    for i in range(3):
        keep = same_image(first_row, height, (2 - i if flip else i) - 1)
        for j in range(3):
            first = 2 - i if flip else i
            second = 2 - j if flip else j
            total = total + full[first : first + height, second : second + across, :] * (
                kernel[i, j] * keep
            )
    return total


def column_taps(padded, kernel, flip, first_row):
    full = padded.astype(jnp.float32)
    height = full.shape[0] - 6
    total = jnp.zeros((height, full.shape[1], full.shape[2]), jnp.float32)
    for i in range(7):
        first = 6 - i if flip else i
        keep = same_image(first_row, height, first - 3)
        total = total + full[first : first + height, :, :] * (kernel[i] * keep)
    return total


def local(
    older_output,
    newer_output,
    output_grad,
    older_weight,
    newer_weight,
    square_point,
    column_point,
    square_kernel,
    column_kernel,
):
    height, across, channels = older_output.shape
    filters = square_point.shape[1]
    shape_three = (height, across, filters)
    first_row = lax.axis_index("rows") * height
    pool_kernel = jnp.full((3, 3, filters), 1.0 / 9.0, jnp.float32)
    older_flat = older_output.reshape(-1, channels)
    newer_flat = newer_output.reshape(-1, channels)
    older_relu = jnp.maximum(older_flat, 0)
    newer_relu = jnp.maximum(newer_flat, 0)
    older_full, newer_full = (
        lax.all_gather(older_weight, "rows", axis=0, tiled=True),
        lax.all_gather(newer_weight, "rows", axis=0, tiled=True),
    )
    older_sum = jnp.dot(older_relu, older_full, preferred_element_type=jnp.float32)
    newer_sum = jnp.dot(newer_relu, newer_full, preferred_element_type=jnp.float32)
    older_mixed = older_sum.astype(jnp.bfloat16).reshape(shape_three)
    newer_mixed = newer_sum.astype(jnp.bfloat16).reshape(shape_three)
    square_full, column_full = (
        lax.all_gather(square_point, "rows", axis=0, tiled=True),
        lax.all_gather(column_point, "rows", axis=0, tiled=True),
    )
    older_rim = with_halo(older_mixed, (("rows", 0),), 3)
    newer_rim = with_halo(newer_mixed, (("rows", 0),), 1)
    square_pre = (
        square_taps(newer_rim, square_kernel, False, first_row)
        .astype(jnp.bfloat16)
        .reshape(-1, filters)
    )
    column_pre = (
        column_taps(older_rim, column_kernel, False, first_row)
        .astype(jnp.bfloat16)
        .reshape(-1, filters)
    )
    pooled = square_taps(older_rim[2:-2], pool_kernel, False, first_row).reshape(-1, filters)
    square_branch = jnp.dot(square_pre, square_full, preferred_element_type=jnp.float32)
    column_branch = jnp.dot(column_pre, column_full, preferred_element_type=jnp.float32)
    cell_output = jnp.concatenate(
        [
            square_branch,
            column_branch,
            pooled,
            newer_mixed.reshape(-1, filters).astype(jnp.float32),
        ],
        axis=1,
    )
    cell_output = cell_output.astype(jnp.bfloat16).reshape(height, across, 4 * filters)
    grads = output_grad.reshape(-1, 4 * filters)
    grad_square = grads[:, :filters]
    grad_column = grads[:, filters : 2 * filters]
    grad_pool = grads[:, 2 * filters : 3 * filters].reshape(shape_three)
    grad_same = grads[:, 3 * filters :].reshape(shape_three)
    square_back = (
        jnp.dot(grad_square, square_full.T, preferred_element_type=jnp.float32)
        .astype(jnp.bfloat16)
        .reshape(shape_three)
    )
    column_back = (
        jnp.dot(grad_column, column_full.T, preferred_element_type=jnp.float32)
        .astype(jnp.bfloat16)
        .reshape(shape_three)
    )
    column_rim = with_halo(column_back, (("rows", 0),), 3)
    square_rim, pool_rim = (
        with_halo(square_back, (("rows", 0),), 1),
        with_halo(grad_pool, (("rows", 0),), 1),
    )
    newer_back = (
        (square_taps(square_rim, square_kernel, True, first_row) + grad_same.astype(jnp.float32))
        .astype(jnp.bfloat16)
        .reshape(-1, filters)
    )
    older_back = (
        (
            column_taps(column_rim, column_kernel, True, first_row)
            + square_taps(pool_rim, pool_kernel, True, first_row)
        )
        .astype(jnp.bfloat16)
        .reshape(-1, filters)
    )
    older_mask = jnp.where(older_flat > 0, 1.0, 0.0).astype(jnp.float32)
    newer_mask = jnp.where(newer_flat > 0, 1.0, 0.0).astype(jnp.float32)
    older_term = jnp.dot(older_back, older_full.T, preferred_element_type=jnp.float32)
    newer_term = jnp.dot(newer_back, newer_full.T, preferred_element_type=jnp.float32)
    older_grad = (older_term * older_mask).astype(jnp.bfloat16).reshape(older_output.shape)
    newer_grad = (newer_term * newer_mask).astype(jnp.bfloat16).reshape(newer_output.shape)
    return (cell_output, older_grad, newer_grad)


def round_up(value, step):
    return -(-value // step) * step


def weight_pieces(shards):
    pieces = []
    for index, shard in enumerate(shards):
        half = shard.shape[0] // 2
        rows = min(half, 64)
        pieces += [(index, at, rows) for at in range(0, half, rows)]
    return pieces


def gather_kernel(count, *refs):
    shards, fulls = refs[:count], refs[count : 2 * count]
    own_sem, y_sems, x_sems, side_sems, pass_sems = refs[2 * count :]
    part, row = lax.axis_index("dp"), lax.axis_index("rows")
    side, across = row + 1 - 2 * (row % 2), (row + 2) % 4
    mate = part + 1 - 2 * (part % 2)
    mine, theirs = part % 2, 1 - part % 2

    barrier = pltpu.get_barrier_semaphore()
    for device in ((part, side), (part, across), (mate, row)):
        pl.semaphore_signal(barrier, inc=1, device_id=device, device_id_type=MESH)
    pl.semaphore_wait(barrier, 3)

    pieces = weight_pieces(shards)

    def span(index, owner, half, at, rows):
        depth = shards[index].shape[0]
        return pl.ds(pl.multiple_of(owner * depth + half * (depth // 2) + at, 64), rows)

    def remote(src, dst, sems, slot, device):
        return pltpu.make_async_remote_copy(
            src_ref=src,
            dst_ref=dst,
            send_sem=sems.at[0, slot],
            recv_sem=sems.at[1, slot],
            device_id=device,
            device_id_type=MESH,
        )

    y_copies, x_copies, low_copies, high_copies = [], [], [], []
    for slot, (index, at, rows) in enumerate(pieces):
        depth = shards[index].shape[0]
        start = pl.ds(pl.multiple_of(mine * (depth // 2) + at, 64), rows)
        sent = fulls[index].at[span(index, row, mine, at, rows)]
        got = fulls[index].at[span(index, across, mine, at, rows)]
        other = fulls[index].at[span(index, across, theirs, at, rows)]
        y_copies.append(remote(shards[index].at[start], sent, y_sems, slot, (part, across)))
        x_copies.append(remote(got, got, x_sems, slot, (mate, row)))
        low_copies.append(remote(got, got, pass_sems, slot, (part, side)))
        high_copies.append(remote(other, other, pass_sems, len(pieces) + slot, (part, side)))
    own_copies, side_copies = [], []
    for index, shard in enumerate(shards):
        depth = shard.shape[0]
        home = fulls[index].at[pl.ds(pl.multiple_of(row * depth, 64), depth)]
        side_copies.append(remote(shard, home, side_sems, index, (part, side)))
        own_copies.append(pltpu.make_async_copy(shard, home, own_sem.at[index]))

    for copy in y_copies + side_copies + own_copies:
        copy.start()
    total = len(pieces)
    for slot in range(total + 1):
        if slot < total:
            y_copies[slot].wait_recv()
            x_copies[slot].start()
            low_copies[slot].start()
        if slot > 0:
            x_copies[slot - 1].wait_recv()
            high_copies[slot - 1].start()
    for copy in low_copies + high_copies + side_copies:
        copy.wait_recv()
    for copy in y_copies + x_copies + low_copies + high_copies + side_copies:
        copy.wait_send()
    for copy in own_copies:
        copy.wait()


def gather_weights(count, *shards):
    total = len(weight_pieces(shards))
    number = len(shards)
    return pl.pallas_call(
        functools.partial(gather_kernel, number),
        out_shape=[
            jax.ShapeDtypeStruct((count * shard.shape[0], shard.shape[1]), shard.dtype)
            for shard in shards
        ],
        in_specs=[pl.BlockSpec(memory_space=pl.ANY)] * number,
        out_specs=[pl.BlockSpec(memory_space=pl.ANY)] * number,
        scratch_shapes=[
            pltpu.SemaphoreType.DMA((number,)),
            pltpu.SemaphoreType.DMA((2, total)),
            pltpu.SemaphoreType.DMA((2, total)),
            pltpu.SemaphoreType.DMA((2, number)),
            pltpu.SemaphoreType.DMA((2, 2 * total)),
        ],
        compiler_params=pltpu.CompilerParams(collective_id=0, has_side_effects=True),
    )(*shards)


def dot_rows(left, right):
    return lax.dot_general(left, right, (((1,), (0,)), ((), ())), preferred_element_type=F32)


def dot_turned(left, right):
    return lax.dot_general(left, right, (((1,), (1,)), ((), ())), preferred_element_type=F32)


def make_shift(tall):
    at = lax.broadcasted_iota(jnp.int32, (tall, LANES), 0)
    at = at % HEIGHT
    keeps = {d: (at + d >= 0) & (at + d < HEIGHT) for d in (-3, -2, -1, 1, 2, 3)}

    def shift(value, d):
        return jnp.where(keeps[d], pltpu.roll(value, (-d) % tall, 0), 0.0)

    return shift


def column_sum(value, taps, flip, shift):
    total = value * taps[3]
    for i in (0, 1, 2, 4, 5, 6):
        total = total + shift(value * taps[i], 3 - i if flip else i - 3)
    return total


def square_sum(low, value, high, taps, flip, shift):
    if flip:
        low, high = high, low
    sums = [low * taps[3 * i] + value * taps[3 * i + 1] + high * taps[3 * i + 2] for i in range(3)]
    if flip:
        sums = sums[::-1]
    return sums[1] + shift(sums[0], -1) + shift(sums[2], 1)


def pool_sum(low, value, high, shift):
    total = low + value + high
    return (total + shift(total, -1) + shift(total, 1)) * (1.0 / 9.0)


def cell_kernel(
    older_hbm,
    newer_hbm,
    grads_hbm,
    older_full,
    newer_full,
    square_full,
    column_full,
    square_taps,
    column_taps,
    cell_hbm,
    older_out_hbm,
    newer_out_hbm,
    older_in,
    newer_in,
    grads_in,
    older_pad,
    newer_pad,
    grads_pad,
    cell_buf,
    older_buf,
    newer_buf,
    rim_a,
    rim_b,
    rim_c,
    back_a,
    back_b,
    in_sems,
    out_sems,
):
    across, height, channels = older_in.shape
    tall = older_pad.shape[1]
    filters = square_full.shape[0]
    wide = across * tall
    tile = min(filters, 256)
    step = filters
    ins = [
        pltpu.make_async_copy(src, dst, in_sems.at[k])
        for k, (src, dst) in enumerate(
            ((grads_hbm, grads_in), (older_hbm, older_in), (newer_hbm, newer_in))
        )
    ]
    for copy in ins:
        copy.start()
    for rim in (rim_a, rim_b):
        rim[0] = jnp.zeros((tall, filters), F32)
        rim[across + 1] = jnp.zeros((tall, filters), F32)
    shift = make_shift(tall)

    def lanes(chunk):
        return pl.ds(pl.multiple_of(chunk * LANES, LANES), LANES)

    def flat(ref, columns):
        return ref[:, :, columns].reshape(wide, columns.size)

    def tiles(body):
        @pl.loop(0, filters // tile)
        def _(n):
            body(pl.multiple_of(n * tile, tile))

    def planes(body):
        @pl.loop(0, filters // LANES)
        def _(chunk):
            @pl.loop(0, across)
            def _(w):
                body(w, lanes(chunk))

    def tap_rows(ref, columns, number):
        return [ref[pl.ds(i, 1), columns] for i in range(number)]

    ins[0].wait()
    grads_pad[:, :height, :] = grads_in[...]

    def back_tile(at):
        cols = pl.ds(at, tile)
        first = dot_turned(flat(grads_pad, pl.ds(0, filters)), square_full[cols, :])
        rim_a[1 : across + 1, :, cols] = first.astype(BF16).astype(F32).reshape(across, tall, tile)
        second = dot_turned(flat(grads_pad, pl.ds(filters, filters)), column_full[cols, :])
        rim_c[:, :, cols] = second.astype(BF16).astype(F32).reshape(across, tall, tile)
        pool_cols = pl.ds(pl.multiple_of(2 * filters + at, tile), tile)
        rim_b[1 : across + 1, :, cols] = grads_pad[:, :, pool_cols].astype(F32)

    tiles(back_tile)

    def back_plane(w, cols):
        taps = tap_rows(square_taps, cols, 9)
        total = square_sum(rim_a[w, :, cols], rim_a[w + 1, :, cols], rim_a[w + 2, :, cols], taps, True, shift)
        same = pl.ds(pl.multiple_of(3 * filters + cols.start, LANES), LANES)
        back_b[w, :, cols] = (total + grads_pad[w, :, same].astype(F32)).astype(BF16)
        total = column_sum(rim_c[w, :, cols], tap_rows(column_taps, cols, 7), True, shift)
        total = total + pool_sum(rim_b[w, :, cols], rim_b[w + 1, :, cols], rim_b[w + 2, :, cols], shift)
        back_a[w, :, cols] = total.astype(BF16)

    planes(back_plane)
    outs = []

    def send(buf, hbm, q):
        cols = pl.ds(q * step, step)
        copy = pltpu.make_async_copy(buf.at[:, :, cols], hbm.at[:, :, cols], out_sems.at[len(outs)])
        copy.start()
        outs.append(copy)

    def grad_blocks(back, full, pad, buf, hbm):
        for q in range(channels // step):
            base = q * step

            def grad_tile(at, base=base):
                cols = pl.ds(pl.multiple_of(base + at, tile), tile)
                term = dot_turned(back[...].reshape(wide, filters), full[cols, :]).reshape(across, tall, tile)
                term = jnp.where(pad[:, :, cols] > 0, term, 0.0)
                buf[:, :, cols] = term[:, :height].astype(BF16)

            tiles(grad_tile)
            send(buf, hbm, q)

    ins[1].wait()
    older_pad[:, :height, :] = jnp.maximum(older_in[...], 0)
    grad_blocks(back_a, older_full, older_pad, older_buf, older_out_hbm)
    ins[2].wait()
    newer_pad[:, :height, :] = jnp.maximum(newer_in[...], 0)
    grad_blocks(back_b, newer_full, newer_pad, newer_buf, newer_out_hbm)

    def mix_tile(at):
        cols = pl.ds(at, tile)
        first = dot_rows(older_pad[...].reshape(wide, channels), older_full[:, cols])
        rim_b[1 : across + 1, :, cols] = first.astype(BF16).astype(F32).reshape(across, tall, tile)
        second = dot_rows(newer_pad[...].reshape(wide, channels), newer_full[:, cols])
        mixed = second.astype(BF16).reshape(across, tall, tile)
        rim_a[1 : across + 1, :, cols] = mixed.astype(F32)
        cell_buf[:, :, pl.ds(pl.multiple_of(3 * filters + at, tile), tile)] = mixed[:, :height]

    tiles(mix_tile)
    send(cell_buf, cell_hbm, 3)

    def mix_plane(w, cols):
        total = square_sum(
            rim_a[w, :, cols], rim_a[w + 1, :, cols], rim_a[w + 2, :, cols], tap_rows(square_taps, cols, 9), False, shift
        )
        back_b[w, :, cols] = total.astype(BF16)
        total = column_sum(rim_b[w + 1, :, cols], tap_rows(column_taps, cols, 7), False, shift)
        back_a[w, :, cols] = total.astype(BF16)
        total = pool_sum(rim_b[w, :, cols], rim_b[w + 1, :, cols], rim_b[w + 2, :, cols], shift)
        pool = pl.ds(pl.multiple_of(2 * filters + cols.start, LANES), LANES)
        cell_buf[w, :, pool] = total[:height].astype(BF16)

    planes(mix_plane)
    send(cell_buf, cell_hbm, 2)

    for q, (back, full) in enumerate(((back_b, square_full), (back_a, column_full))):

        def point_tile(at, q=q, back=back, full=full):
            term = dot_rows(back[...].reshape(wide, filters), full[:, pl.ds(at, tile)])
            cols = pl.ds(pl.multiple_of(q * filters + at, tile), tile)
            cell_buf[:, :, cols] = term.reshape(across, tall, tile)[:, :height].astype(BF16)

        tiles(point_tile)
        send(cell_buf, cell_hbm, q)
    for copy in outs:
        copy.wait()


def cell(older, newer, grads, older_full, newer_full, square_full, column_full, square_taps, column_taps):
    across, height, channels = older.shape
    filters = square_full.shape[0]
    tall = round_up(height, 16)
    plain = pltpu.VMEM((across, height, channels), BF16)
    padded = pltpu.VMEM((across, tall, channels), BF16)
    rim = pltpu.VMEM((across + 2, tall, filters), F32)
    back = pltpu.VMEM((across, tall, filters), BF16)
    anywhere = pl.BlockSpec(memory_space=pl.ANY)
    inside = pl.BlockSpec(memory_space=pltpu.VMEM)
    blocks = 2 * (channels // filters) + 4
    return pl.pallas_call(
        cell_kernel,
        out_shape=[jax.ShapeDtypeStruct(older.shape, BF16)] * 3,
        in_specs=[anywhere] * 3 + [inside] * 6,
        out_specs=[anywhere] * 3,
        scratch_shapes=[plain] * 3
        + [padded] * 3
        + [plain] * 3
        + [rim, rim, pltpu.VMEM((across, tall, filters), F32), back, back]
        + [pltpu.SemaphoreType.DMA((3,)), pltpu.SemaphoreType.DMA((blocks,))],
        compiler_params=pltpu.CompilerParams(vmem_limit_bytes=60 * 1024 * 1024),
        name="cell",
    )(older, newer, grads, older_full, newer_full, square_full, column_full, square_taps, column_taps)


def whole_images(
    older_output,
    newer_output,
    output_grad,
    older_weight,
    newer_weight,
    square_point,
    column_point,
    square_kernel,
    column_kernel,
):
    count = lax.axis_size("rows")
    square_full, column_full, older_full, newer_full = gather_weights(
        count, square_point, column_point, older_weight, newer_weight
    )
    filters = square_point.shape[1]
    outs = cell(
        *(jnp.transpose(x, (1, 0, 2)) for x in (older_output, newer_output, output_grad)),
        older_full,
        newer_full,
        square_full,
        column_full,
        square_kernel.reshape(9, filters),
        column_kernel,
    )
    return tuple(jnp.transpose(x, (1, 0, 2)) for x in outs)


def choose(*arrays):
    height = arrays[0].shape[0]
    routes = lax.axis_size("rows") == 4 and lax.axis_size("dp") % 2 == 0
    if height % HEIGHT == 0 and routes:
        return whole_images(*arrays)
    return local(*arrays)


def solution(mesh):
    in_specs = (
        P(("dp", "rows"), None, None),
        P(("dp", "rows"), None, None),
        P(("dp", "rows"), None, None),
        P("rows", None),
        P("rows", None),
        P("rows", None),
        P("rows", None),
        P(),
        P(),
    )
    out_specs = (
        P(("dp", "rows"), None, None),
        P(("dp", "rows"), None, None),
        P(("dp", "rows"), None, None),
    )
    return jax.shard_map(choose, mesh=mesh, in_specs=in_specs, out_specs=out_specs, check_vma=False)
```

```python
import jax
import jax.numpy as jnp
from jax import lax
from jax.experimental import pallas as pl
from jax.experimental.pallas import tpu as pltpu
from jax.sharding import PartitionSpec as P

MESH = pl.DeviceIdType.MESH
F32 = jnp.float32
BF16 = jnp.bfloat16
LANES = 128

HEIGHT = 30


def with_halo(block, sides, width):
    for axis, dim in sides:
        count = lax.axis_size(axis)
        forward = [(i, i + 1) for i in range(count - 1)]
        backward = [(target, source) for source, target in forward]
        low = lax.ppermute(
            lax.slice_in_dim(block, block.shape[dim] - width, None, axis=dim), axis, forward
        )
        high = lax.ppermute(lax.slice_in_dim(block, 0, width, axis=dim), axis, backward)
        block = jnp.concatenate([low, block, high], axis=dim)
    return block


def same_image(first_row, local_rows, offset):
    row_ids = jnp.arange(local_rows, dtype=jnp.int32) + first_row
    inside = jnp.floor_divide(row_ids + offset, HEIGHT) == jnp.floor_divide(row_ids, HEIGHT)
    return jnp.where(inside, 1.0, 0.0).astype(jnp.float32)[:, None, None]


def square_taps(padded, kernel, flip, first_row):
    full = jnp.pad(padded, ((0, 0), (1, 1), (0, 0))).astype(jnp.float32)
    height = full.shape[0] - 2
    across = full.shape[1] - 2
    total = jnp.zeros((height, across, full.shape[2]), jnp.float32)
    for i in range(3):
        keep = same_image(first_row, height, (2 - i if flip else i) - 1)
        for j in range(3):
            first = 2 - i if flip else i
            second = 2 - j if flip else j
            total = total + full[first : first + height, second : second + across, :] * (
                kernel[i, j] * keep
            )
    return total


def column_taps(padded, kernel, flip, first_row):
    full = padded.astype(jnp.float32)
    height = full.shape[0] - 6
    total = jnp.zeros((height, full.shape[1], full.shape[2]), jnp.float32)
    for i in range(7):
        first = 6 - i if flip else i
        keep = same_image(first_row, height, first - 3)
        total = total + full[first : first + height, :, :] * (kernel[i] * keep)
    return total


def local(
    older_output,
    newer_output,
    output_grad,
    older_weight,
    newer_weight,
    square_point,
    column_point,
    square_kernel,
    column_kernel,
):
    height, across, channels = older_output.shape
    filters = square_point.shape[1]
    shape_three = (height, across, filters)
    first_row = lax.axis_index("rows") * height
    pool_kernel = jnp.full((3, 3, filters), 1.0 / 9.0, jnp.float32)
    older_flat = older_output.reshape(-1, channels)
    newer_flat = newer_output.reshape(-1, channels)
    older_relu = jnp.maximum(older_flat, 0)
    newer_relu = jnp.maximum(newer_flat, 0)
    older_full, newer_full = (
        lax.all_gather(older_weight, "rows", axis=0, tiled=True),
        lax.all_gather(newer_weight, "rows", axis=0, tiled=True),
    )
    older_sum = jnp.dot(older_relu, older_full, preferred_element_type=jnp.float32)
    newer_sum = jnp.dot(newer_relu, newer_full, preferred_element_type=jnp.float32)
    older_mixed = older_sum.astype(jnp.bfloat16).reshape(shape_three)
    newer_mixed = newer_sum.astype(jnp.bfloat16).reshape(shape_three)
    square_full, column_full = (
        lax.all_gather(square_point, "rows", axis=0, tiled=True),
        lax.all_gather(column_point, "rows", axis=0, tiled=True),
    )
    older_rim = with_halo(older_mixed, (("rows", 0),), 3)
    newer_rim = with_halo(newer_mixed, (("rows", 0),), 1)
    square_pre = (
        square_taps(newer_rim, square_kernel, False, first_row)
        .astype(jnp.bfloat16)
        .reshape(-1, filters)
    )
    column_pre = (
        column_taps(older_rim, column_kernel, False, first_row)
        .astype(jnp.bfloat16)
        .reshape(-1, filters)
    )
    pooled = square_taps(older_rim[2:-2], pool_kernel, False, first_row).reshape(-1, filters)
    square_branch = jnp.dot(square_pre, square_full, preferred_element_type=jnp.float32)
    column_branch = jnp.dot(column_pre, column_full, preferred_element_type=jnp.float32)
    cell_output = jnp.concatenate(
        [
            square_branch,
            column_branch,
            pooled,
            newer_mixed.reshape(-1, filters).astype(jnp.float32),
        ],
        axis=1,
    )
    cell_output = cell_output.astype(jnp.bfloat16).reshape(height, across, 4 * filters)
    grads = output_grad.reshape(-1, 4 * filters)
    grad_square = grads[:, :filters]
    grad_column = grads[:, filters : 2 * filters]
    grad_pool = grads[:, 2 * filters : 3 * filters].reshape(shape_three)
    grad_same = grads[:, 3 * filters :].reshape(shape_three)
    square_back = (
        jnp.dot(grad_square, square_full.T, preferred_element_type=jnp.float32)
        .astype(jnp.bfloat16)
        .reshape(shape_three)
    )
    column_back = (
        jnp.dot(grad_column, column_full.T, preferred_element_type=jnp.float32)
        .astype(jnp.bfloat16)
        .reshape(shape_three)
    )
    column_rim = with_halo(column_back, (("rows", 0),), 3)
    square_rim, pool_rim = (
        with_halo(square_back, (("rows", 0),), 1),
        with_halo(grad_pool, (("rows", 0),), 1),
    )
    newer_back = (
        (square_taps(square_rim, square_kernel, True, first_row) + grad_same.astype(jnp.float32))
        .astype(jnp.bfloat16)
        .reshape(-1, filters)
    )
    older_back = (
        (
            column_taps(column_rim, column_kernel, True, first_row)
            + square_taps(pool_rim, pool_kernel, True, first_row)
        )
        .astype(jnp.bfloat16)
        .reshape(-1, filters)
    )
    older_mask = jnp.where(older_flat > 0, 1.0, 0.0).astype(jnp.float32)
    newer_mask = jnp.where(newer_flat > 0, 1.0, 0.0).astype(jnp.float32)
    older_term = jnp.dot(older_back, older_full.T, preferred_element_type=jnp.float32)
    newer_term = jnp.dot(newer_back, newer_full.T, preferred_element_type=jnp.float32)
    older_grad = (older_term * older_mask).astype(jnp.bfloat16).reshape(older_output.shape)
    newer_grad = (newer_term * newer_mask).astype(jnp.bfloat16).reshape(newer_output.shape)
    return (cell_output, older_grad, newer_grad)


def round_up(value, step):
    return -(-value // step) * step


def weight_pieces(shards):
    pieces = []
    for index, shard in enumerate(shards):
        half = shard.shape[0] // 2
        rows = min(half, 128)
        pieces += [(index, at, rows) for at in range(0, half, rows)]
    return pieces


class Exchange:
    def __init__(self, shards, fulls, own_sem, y_sems, x_sems, side_sems, pass_sems):
        part, row = lax.axis_index("dp"), lax.axis_index("rows")
        side, across = row + 1 - 2 * (row % 2), (row + 2) % 4
        mate = part + 1 - 2 * (part % 2)
        mine, theirs = part % 2, 1 - part % 2
        barrier = pltpu.get_barrier_semaphore()
        for device in ((part, side), (part, across), (mate, row)):
            pl.semaphore_signal(barrier, inc=1, device_id=device, device_id_type=MESH)
        pl.semaphore_wait(barrier, 3)
        self.pieces = weight_pieces(shards)

        def span(index, owner, half, at, rows):
            depth = shards[index].shape[0]
            return pl.ds(pl.multiple_of(owner * depth + half * (depth // 2) + at, 64), rows)

        def remote(src, dst, sems, slot, device):
            return pltpu.make_async_remote_copy(
                src_ref=src,
                dst_ref=dst,
                send_sem=sems.at[0, slot],
                recv_sem=sems.at[1, slot],
                device_id=device,
                device_id_type=MESH,
            )

        self.y, self.x, self.low, self.high, self.own, self.side = [], [], [], [], [], []
        total = len(self.pieces)
        for slot, (index, at, rows) in enumerate(self.pieces):
            depth = shards[index].shape[0]
            start = pl.ds(pl.multiple_of(mine * (depth // 2) + at, 64), rows)
            sent = fulls[index].at[span(index, row, mine, at, rows)]
            got = fulls[index].at[span(index, across, mine, at, rows)]
            other = fulls[index].at[span(index, across, theirs, at, rows)]
            self.y.append(remote(shards[index].at[start], sent, y_sems, slot, (part, across)))
            self.x.append(remote(got, got, x_sems, slot, (mate, row)))
            self.low.append(remote(got, got, pass_sems, slot, (part, side)))
            self.high.append(remote(other, other, pass_sems, total + slot, (part, side)))
        for index, shard in enumerate(shards):
            depth = shard.shape[0]
            home = fulls[index].at[pl.ds(pl.multiple_of(row * depth, 64), depth)]
            self.side.append(remote(shard, home, side_sems, index, (part, side)))
            self.own.append(pltpu.make_async_copy(shard, home, own_sem.at[index]))
        for copy in self.y + self.side + self.own:
            copy.start()

    def forward(self, slot):
        if slot < len(self.pieces):
            self.y[slot].wait_recv()
            self.x[slot].start()
            self.low[slot].start()
        if slot > 0:
            self.x[slot - 1].wait_recv()
            self.high[slot - 1].start()

    def wait_array(self, index):
        for slot, piece in enumerate(self.pieces):
            if piece[0] == index:
                self.low[slot].wait_recv()
                self.high[slot].wait_recv()
        self.side[index].wait_recv()
        self.own[index].wait()

    def finish(self):
        for copy in self.y + self.x + self.low + self.high + self.side:
            copy.wait_send()


def exchange_semaphores(shards):
    total, number = len(weight_pieces(shards)), len(shards)
    return [
        pltpu.SemaphoreType.DMA((number,)),
        pltpu.SemaphoreType.DMA((2, total)),
        pltpu.SemaphoreType.DMA((2, total)),
        pltpu.SemaphoreType.DMA((2, number)),
        pltpu.SemaphoreType.DMA((2, 2 * total)),
    ]


def dot_rows(left, right):
    return lax.dot_general(left, right, (((1,), (0,)), ((), ())), preferred_element_type=F32)


def dot_turned(left, right):
    return lax.dot_general(left, right, (((1,), (1,)), ((), ())), preferred_element_type=F32)


def make_shift(tall):
    at = lax.broadcasted_iota(jnp.int32, (tall, LANES), 0)
    at = at % HEIGHT
    keeps = {d: (at + d >= 0) & (at + d < HEIGHT) for d in (-3, -2, -1, 1, 2, 3)}

    def shift(value, d):
        return jnp.where(keeps[d], pltpu.roll(value, (-d) % tall, 0), 0.0)

    return shift


def column_sum(value, taps, flip, shift):
    total = value * taps[3]
    for i in (0, 1, 2, 4, 5, 6):
        total = total + shift(value * taps[i], 3 - i if flip else i - 3)
    return total


def square_sum(low, value, high, taps, flip, shift):
    if flip:
        low, high = high, low
    sums = [low * taps[3 * i] + value * taps[3 * i + 1] + high * taps[3 * i + 2] for i in range(3)]
    if flip:
        sums = sums[::-1]
    return sums[1] + shift(sums[0], -1) + shift(sums[2], 1)


def pool_sum(low, value, high, shift):
    total = low + value + high
    return (total + shift(total, -1) + shift(total, 1)) * (1.0 / 9.0)


def lanes(chunk):
    return pl.ds(pl.multiple_of(chunk * LANES, LANES), LANES)


def flat(ref, columns):
    across, tall, _ = ref.shape
    return ref[:, :, columns].reshape(across * tall, columns.size)


def tiles(filters, tile, body):
    @pl.loop(0, filters // tile)
    def _(n):
        body(pl.multiple_of(n * tile, tile))


def planes(first, last, across, body):
    @pl.loop(first, last)
    def _(chunk):
        @pl.loop(0, across)
        def _(w):
            body(w, lanes(chunk))


def tap_rows(ref, columns, number):
    return [ref[pl.ds(i, 1), columns] for i in range(number)]


def clear_ends(rim):
    rim[0] = jnp.zeros(rim.shape[1:], F32)
    rim[rim.shape[0] - 1] = jnp.zeros(rim.shape[1:], F32)


def early_kernel(
    older_hbm,
    grads_hbm,
    square_shard,
    column_shard,
    older_shard,
    square_taps,
    column_taps,
    back_a,
    back_b,
    branch,
    square_hbm,
    older_full_hbm,
    older_in,
    grads_in,
    older_pad,
    grads_pad,
    square_full,
    column_full,
    older_full,
    rim_a,
    rim_b,
    rim_c,
    pre,
    in_sems,
    out_sems,
    *exchange_sems,
):
    across, height, channels = older_in.shape
    tall = older_pad.shape[1]
    filters = square_full.shape[0]
    wide = across * tall
    tile = min(filters, 256)
    chunks = filters // LANES
    ins = [
        pltpu.make_async_copy(grads_hbm, grads_in, in_sems.at[0]),
        pltpu.make_async_copy(older_hbm, older_in, in_sems.at[1]),
    ]
    for copy in ins:
        copy.start()
    trade = Exchange(
        (square_shard, column_shard, older_shard),
        (square_full, column_full, older_full),
        *exchange_sems,
    )
    last = len(trade.pieces)
    clear_ends(rim_a)
    clear_ends(rim_b)
    shift = make_shift(tall)
    ins[0].wait()
    grads_pad[:, :height, :] = grads_in[...]
    trade.forward(0)
    trade.forward(1)
    ins[1].wait()
    older_pad[:, :height, :] = jnp.maximum(older_in[...], 0)
    trade.forward(2)
    trade.wait_array(0)
    trade.wait_array(1)

    def back_tile(at):
        cols = pl.ds(at, tile)
        first = dot_turned(flat(grads_pad, pl.ds(0, filters)), square_full[cols, :])
        rim_a[1 : across + 1, :, cols] = first.astype(BF16).astype(F32).reshape(across, tall, tile)
        second = dot_turned(flat(grads_pad, pl.ds(filters, filters)), column_full[cols, :])
        rim_c[:, :, cols] = second.astype(BF16).astype(F32).reshape(across, tall, tile)
        pool_cols = pl.ds(pl.multiple_of(2 * filters + at, tile), tile)
        rim_b[1 : across + 1, :, cols] = grads_pad[:, :, pool_cols].astype(F32)

    tiles(filters, tile, back_tile)

    def back_plane(w, cols):
        taps = tap_rows(square_taps, cols, 9)
        total = square_sum(rim_a[w, :, cols], rim_a[w + 1, :, cols], rim_a[w + 2, :, cols], taps, True, shift)
        same = pl.ds(pl.multiple_of(3 * filters + cols.start, LANES), LANES)
        back_b[w, :, cols] = (total + grads_pad[w, :, same].astype(F32)).astype(BF16)
        total = column_sum(rim_c[w, :, cols], tap_rows(column_taps, cols, 7), True, shift)
        total = total + pool_sum(rim_b[w, :, cols], rim_b[w + 1, :, cols], rim_b[w + 2, :, cols], shift)
        back_a[w, :, cols] = total.astype(BF16)

    done = 0
    for slot in range(3, last + 1):
        until = (slot - 2) * chunks // max(1, last - 2)
        planes(done, until, across, back_plane)
        done = until
        trade.forward(slot)
    if done < chunks:
        planes(done, chunks, across, back_plane)
    trade.wait_array(2)
    outs = [
        pltpu.make_async_copy(square_full, square_hbm, out_sems.at[0]),
        pltpu.make_async_copy(older_full, older_full_hbm, out_sems.at[1]),
    ]
    for copy in outs:
        copy.start()

    def mix_tile(at):
        cols = pl.ds(at, tile)
        mixed = dot_rows(older_pad[...].reshape(wide, channels), older_full[:, cols])
        rim_b[1 : across + 1, :, cols] = mixed.astype(BF16).astype(F32).reshape(across, tall, tile)

    tiles(filters, tile, mix_tile)

    def mix_plane(w, cols):
        total = column_sum(rim_b[w + 1, :, cols], tap_rows(column_taps, cols, 7), False, shift)
        pre[w, :, cols] = total.astype(BF16)
        total = pool_sum(rim_b[w, :, cols], rim_b[w + 1, :, cols], rim_b[w + 2, :, cols], shift)
        pool = pl.ds(pl.multiple_of(filters + cols.start, LANES), LANES)
        branch[w, :, pool] = total[:height].astype(BF16)

    planes(0, chunks, across, mix_plane)

    def point_tile(at):
        cols = pl.ds(at, tile)
        term = dot_rows(pre[...].reshape(wide, filters), column_full[:, cols])
        branch[:, :, cols] = term.reshape(across, tall, tile)[:, :height].astype(BF16)

    tiles(filters, tile, point_tile)
    trade.finish()
    for copy in outs:
        copy.wait()


def early(older, grads, square_shard, column_shard, older_shard, square_taps, column_taps, count):
    across, height, channels = older.shape
    filters = square_shard.shape[1]
    tall = round_up(height, 16)
    plain = pltpu.VMEM((across, height, channels), BF16)
    padded = pltpu.VMEM((across, tall, channels), BF16)
    rim = pltpu.VMEM((across + 2, tall, filters), F32)
    shards = (square_shard, column_shard, older_shard)
    fulls = [(count * x.shape[0], x.shape[1]) for x in shards]
    anywhere = pl.BlockSpec(memory_space=pl.ANY)
    inside = pl.BlockSpec(memory_space=pltpu.VMEM)
    back = jax.ShapeDtypeStruct((across, tall, filters), BF16)
    flops = 2 * across * tall * filters * (channels + 3 * filters)
    return pl.pallas_call(
        early_kernel,
        out_shape=[
            back,
            back,
            jax.ShapeDtypeStruct((across, height, 2 * filters), BF16),
            jax.ShapeDtypeStruct(fulls[0], BF16),
            jax.ShapeDtypeStruct(fulls[2], BF16),
        ],
        in_specs=[anywhere] * 5 + [inside] * 2,
        out_specs=[inside] * 3 + [anywhere] * 2,
        scratch_shapes=[plain, plain, padded, padded]
        + [pltpu.VMEM(shape, BF16) for shape in fulls]
        + [rim, rim, pltpu.VMEM((across, tall, filters), F32)]
        + [pltpu.VMEM((across, tall, filters), BF16)]
        + [pltpu.SemaphoreType.DMA((2,)), pltpu.SemaphoreType.DMA((2,))]
        + exchange_semaphores(shards),
        compiler_params=pltpu.CompilerParams(
            collective_id=0, has_side_effects=True, vmem_limit_bytes=48 * 1024 * 1024
        ),
        cost_estimate=pl.CostEstimate(flops=flops, bytes_accessed=20 * older.size, transcendentals=0),
        name="early",
    )(older, grads, *shards, square_taps, column_taps)


def grad_blocks(back, full, pad, buf, hbm, sems, height):
    across, tall, filters = back.shape
    channels = full.shape[0]
    tile = min(filters, 256)
    outs = []
    for q in range(channels // filters):

        def grad_tile(at, base=q * filters):
            cols = pl.ds(pl.multiple_of(base + at, tile), tile)
            term = dot_turned(back[...].reshape(across * tall, filters), full[cols, :])
            term = jnp.where(pad[:, :, cols] > 0, term.reshape(across, tall, tile), 0.0)
            buf[:, :, cols] = term[:, :height].astype(BF16)

        tiles(filters, tile, grad_tile)
        cols = pl.ds(q * filters, filters)
        outs.append(pltpu.make_async_copy(buf.at[:, :, cols], hbm.at[:, :, cols], sems.at[q]))
        outs[-1].start()
    return outs


def older_kernel(older_hbm, back, full, out_hbm, older_in, pad, buf, in_sem, out_sems):
    height = older_in.shape[1]
    load = pltpu.make_async_copy(older_hbm, older_in, in_sem)
    load.start()
    load.wait()
    pad[:, :height, :] = older_in[...]
    for copy in grad_blocks(back, full, pad, buf, out_hbm, out_sems, height):
        copy.wait()


def older_part(older, back, full):
    across, height, channels = older.shape
    tall, filters = back.shape[1:]
    plain = pltpu.VMEM(older.shape, BF16)
    anywhere = pl.BlockSpec(memory_space=pl.ANY)
    inside = pl.BlockSpec(memory_space=pltpu.VMEM)
    return pl.pallas_call(
        older_kernel,
        out_shape=jax.ShapeDtypeStruct(older.shape, BF16),
        in_specs=[anywhere, inside, inside],
        out_specs=anywhere,
        scratch_shapes=[plain, pltpu.VMEM((across, tall, channels), BF16), plain]
        + [pltpu.SemaphoreType.DMA(()), pltpu.SemaphoreType.DMA((channels // filters,))],
        compiler_params=pltpu.CompilerParams(vmem_limit_bytes=40 * 1024 * 1024),
        cost_estimate=pl.CostEstimate(
            flops=2 * across * tall * filters * channels, bytes_accessed=6 * older.size, transcendentals=0
        ),
        name="older",
    )(older, back, full)


def newer_kernel(
    newer_hbm,
    branch_hbm,
    back,
    newer_full,
    square_full,
    square_taps,
    cell_hbm,
    out_hbm,
    newer_in,
    pad,
    buf,
    cell_buf,
    rim,
    pre,
    in_sems,
    out_sems,
    grad_sems,
):
    across, height, channels = newer_in.shape
    tall = pad.shape[1]
    filters = square_full.shape[0]
    wide = across * tall
    tile = min(filters, 256)
    load = pltpu.make_async_copy(newer_hbm, newer_in, in_sems.at[0])
    load.start()
    middle = pl.ds(filters, 2 * filters)
    fetch = pltpu.make_async_copy(branch_hbm, cell_buf.at[:, :, middle], in_sems.at[1])
    fetch.start()
    clear_ends(rim)
    shift = make_shift(tall)
    load.wait()
    pad[:, :height, :] = jnp.maximum(newer_in[...], 0)
    outs = grad_blocks(back, newer_full, pad, buf, out_hbm, grad_sems, height)
    fetch.wait()

    def send(columns, slot):
        copy = pltpu.make_async_copy(cell_buf.at[:, :, columns], cell_hbm.at[:, :, columns], out_sems.at[slot])
        copy.start()
        outs.append(copy)

    send(middle, 0)

    def mix_tile(at):
        cols = pl.ds(at, tile)
        total = dot_rows(pad[...].reshape(wide, channels), newer_full[:, cols])
        mixed = total.astype(BF16).reshape(across, tall, tile)
        rim[1 : across + 1, :, cols] = mixed.astype(F32)
        cell_buf[:, :, pl.ds(pl.multiple_of(3 * filters + at, tile), tile)] = mixed[:, :height]

    tiles(filters, tile, mix_tile)
    send(pl.ds(3 * filters, filters), 1)

    def mix_plane(w, cols):
        taps = tap_rows(square_taps, cols, 9)
        total = square_sum(rim[w, :, cols], rim[w + 1, :, cols], rim[w + 2, :, cols], taps, False, shift)
        pre[w, :, cols] = total.astype(BF16)

    planes(0, filters // LANES, across, mix_plane)

    def point_tile(at):
        cols = pl.ds(at, tile)
        term = dot_rows(pre[...].reshape(wide, filters), square_full[:, cols])
        cell_buf[:, :, cols] = term.reshape(across, tall, tile)[:, :height].astype(BF16)

    tiles(filters, tile, point_tile)
    send(pl.ds(0, filters), 2)
    for copy in outs:
        copy.wait()


def newer_part(newer, branch, back, newer_full, square_full, square_taps):
    across, height, channels = newer.shape
    tall, filters = back.shape[1:]
    plain = pltpu.VMEM(newer.shape, BF16)
    anywhere = pl.BlockSpec(memory_space=pl.ANY)
    inside = pl.BlockSpec(memory_space=pltpu.VMEM)
    return pl.pallas_call(
        newer_kernel,
        out_shape=[jax.ShapeDtypeStruct(newer.shape, BF16)] * 2,
        in_specs=[anywhere] * 2 + [inside] * 4,
        out_specs=[anywhere] * 2,
        scratch_shapes=[plain, pltpu.VMEM((across, tall, channels), BF16), plain, plain]
        + [pltpu.VMEM((across + 2, tall, filters), F32), pltpu.VMEM((across, tall, filters), BF16)]
        + [pltpu.SemaphoreType.DMA((2,)), pltpu.SemaphoreType.DMA((3,))]
        + [pltpu.SemaphoreType.DMA((channels // filters,))],
        compiler_params=pltpu.CompilerParams(vmem_limit_bytes=48 * 1024 * 1024),
        name="newer",
    )(newer, branch, back, newer_full, square_full, square_taps)


def whole_images(
    older_output,
    newer_output,
    output_grad,
    older_weight,
    newer_weight,
    square_point,
    column_point,
    square_kernel,
    column_kernel,
):
    count = lax.axis_size("rows")
    filters = square_point.shape[1]
    newer_full = lax.all_gather(newer_weight, "rows", axis=0, tiled=True)
    older, newer, grads = (jnp.transpose(x, (1, 0, 2)) for x in (older_output, newer_output, output_grad))
    square_taps = square_kernel.reshape(9, filters)
    back_a, back_b, branch, square_full, older_full = early(
        older, grads, square_point, column_point, older_weight, square_taps, column_kernel, count
    )
    older_grad = older_part(older, back_a, older_full)
    cell_output, newer_grad = newer_part(newer, branch, back_b, newer_full, square_full, square_taps)
    return tuple(jnp.transpose(x, (1, 0, 2)) for x in (cell_output, older_grad, newer_grad))


def choose(*arrays):
    height = arrays[0].shape[0]
    routes = lax.axis_size("rows") == 4 and lax.axis_size("dp") % 2 == 0
    if height % HEIGHT == 0 and routes:
        return whole_images(*arrays)
    return local(*arrays)


def solution(mesh):
    in_specs = (
        P(("dp", "rows"), None, None),
        P(("dp", "rows"), None, None),
        P(("dp", "rows"), None, None),
        P("rows", None),
        P("rows", None),
        P("rows", None),
        P("rows", None),
        P(),
        P(),
    )
    out_specs = (
        P(("dp", "rows"), None, None),
        P(("dp", "rows"), None, None),
        P(("dp", "rows"), None, None),
    )
    return jax.shard_map(choose, mesh=mesh, in_specs=in_specs, out_specs=out_specs, check_vma=False)
```

```python
import jax
import jax.numpy as jnp
from jax import lax
from jax.experimental import pallas as pl
from jax.experimental.pallas import tpu as pltpu
from jax.sharding import PartitionSpec as P

MESH = pl.DeviceIdType.MESH
F32 = jnp.float32
BF16 = jnp.bfloat16
LANES = 128

HEIGHT = 30


def with_halo(block, sides, width):
    for axis, dim in sides:
        count = lax.axis_size(axis)
        forward = [(i, i + 1) for i in range(count - 1)]
        backward = [(target, source) for source, target in forward]
        low = lax.ppermute(
            lax.slice_in_dim(block, block.shape[dim] - width, None, axis=dim), axis, forward
        )
        high = lax.ppermute(lax.slice_in_dim(block, 0, width, axis=dim), axis, backward)
        block = jnp.concatenate([low, block, high], axis=dim)
    return block


def same_image(first_row, local_rows, offset):
    row_ids = jnp.arange(local_rows, dtype=jnp.int32) + first_row
    inside = jnp.floor_divide(row_ids + offset, HEIGHT) == jnp.floor_divide(row_ids, HEIGHT)
    return jnp.where(inside, 1.0, 0.0).astype(jnp.float32)[:, None, None]


def square_taps(padded, kernel, flip, first_row):
    full = jnp.pad(padded, ((0, 0), (1, 1), (0, 0))).astype(jnp.float32)
    height = full.shape[0] - 2
    across = full.shape[1] - 2
    total = jnp.zeros((height, across, full.shape[2]), jnp.float32)
    for i in range(3):
        keep = same_image(first_row, height, (2 - i if flip else i) - 1)
        for j in range(3):
            first = 2 - i if flip else i
            second = 2 - j if flip else j
            total = total + full[first : first + height, second : second + across, :] * (
                kernel[i, j] * keep
            )
    return total


def column_taps(padded, kernel, flip, first_row):
    full = padded.astype(jnp.float32)
    height = full.shape[0] - 6
    total = jnp.zeros((height, full.shape[1], full.shape[2]), jnp.float32)
    for i in range(7):
        first = 6 - i if flip else i
        keep = same_image(first_row, height, first - 3)
        total = total + full[first : first + height, :, :] * (kernel[i] * keep)
    return total


def local(
    older_output,
    newer_output,
    output_grad,
    older_weight,
    newer_weight,
    square_point,
    column_point,
    square_kernel,
    column_kernel,
):
    height, across, channels = older_output.shape
    filters = square_point.shape[1]
    shape_three = (height, across, filters)
    first_row = lax.axis_index("rows") * height
    pool_kernel = jnp.full((3, 3, filters), 1.0 / 9.0, jnp.float32)
    older_flat = older_output.reshape(-1, channels)
    newer_flat = newer_output.reshape(-1, channels)
    older_relu = jnp.maximum(older_flat, 0)
    newer_relu = jnp.maximum(newer_flat, 0)
    older_full, newer_full = (
        lax.all_gather(older_weight, "rows", axis=0, tiled=True),
        lax.all_gather(newer_weight, "rows", axis=0, tiled=True),
    )
    older_sum = jnp.dot(older_relu, older_full, preferred_element_type=jnp.float32)
    newer_sum = jnp.dot(newer_relu, newer_full, preferred_element_type=jnp.float32)
    older_mixed = older_sum.astype(jnp.bfloat16).reshape(shape_three)
    newer_mixed = newer_sum.astype(jnp.bfloat16).reshape(shape_three)
    square_full, column_full = (
        lax.all_gather(square_point, "rows", axis=0, tiled=True),
        lax.all_gather(column_point, "rows", axis=0, tiled=True),
    )
    older_rim = with_halo(older_mixed, (("rows", 0),), 3)
    newer_rim = with_halo(newer_mixed, (("rows", 0),), 1)
    square_pre = (
        square_taps(newer_rim, square_kernel, False, first_row)
        .astype(jnp.bfloat16)
        .reshape(-1, filters)
    )
    column_pre = (
        column_taps(older_rim, column_kernel, False, first_row)
        .astype(jnp.bfloat16)
        .reshape(-1, filters)
    )
    pooled = square_taps(older_rim[2:-2], pool_kernel, False, first_row).reshape(-1, filters)
    square_branch = jnp.dot(square_pre, square_full, preferred_element_type=jnp.float32)
    column_branch = jnp.dot(column_pre, column_full, preferred_element_type=jnp.float32)
    cell_output = jnp.concatenate(
        [
            square_branch,
            column_branch,
            pooled,
            newer_mixed.reshape(-1, filters).astype(jnp.float32),
        ],
        axis=1,
    )
    cell_output = cell_output.astype(jnp.bfloat16).reshape(height, across, 4 * filters)
    grads = output_grad.reshape(-1, 4 * filters)
    grad_square = grads[:, :filters]
    grad_column = grads[:, filters : 2 * filters]
    grad_pool = grads[:, 2 * filters : 3 * filters].reshape(shape_three)
    grad_same = grads[:, 3 * filters :].reshape(shape_three)
    square_back = (
        jnp.dot(grad_square, square_full.T, preferred_element_type=jnp.float32)
        .astype(jnp.bfloat16)
        .reshape(shape_three)
    )
    column_back = (
        jnp.dot(grad_column, column_full.T, preferred_element_type=jnp.float32)
        .astype(jnp.bfloat16)
        .reshape(shape_three)
    )
    column_rim = with_halo(column_back, (("rows", 0),), 3)
    square_rim, pool_rim = (
        with_halo(square_back, (("rows", 0),), 1),
        with_halo(grad_pool, (("rows", 0),), 1),
    )
    newer_back = (
        (square_taps(square_rim, square_kernel, True, first_row) + grad_same.astype(jnp.float32))
        .astype(jnp.bfloat16)
        .reshape(-1, filters)
    )
    older_back = (
        (
            column_taps(column_rim, column_kernel, True, first_row)
            + square_taps(pool_rim, pool_kernel, True, first_row)
        )
        .astype(jnp.bfloat16)
        .reshape(-1, filters)
    )
    older_mask = jnp.where(older_flat > 0, 1.0, 0.0).astype(jnp.float32)
    newer_mask = jnp.where(newer_flat > 0, 1.0, 0.0).astype(jnp.float32)
    older_term = jnp.dot(older_back, older_full.T, preferred_element_type=jnp.float32)
    newer_term = jnp.dot(newer_back, newer_full.T, preferred_element_type=jnp.float32)
    older_grad = (older_term * older_mask).astype(jnp.bfloat16).reshape(older_output.shape)
    newer_grad = (newer_term * newer_mask).astype(jnp.bfloat16).reshape(newer_output.shape)
    return (cell_output, older_grad, newer_grad)


def round_up(value, step):
    return -(-value // step) * step


def weight_pieces(shards):
    pieces = []
    for index, shard in enumerate(shards):
        half = shard.shape[0] // 2
        rows = min(half, 128)
        pieces += [(index, at, rows) for at in range(0, half, rows)]
    return pieces


class Exchange:
    def __init__(self, shards, fulls, own_sem, y_sems, x_sems, side_sems):
        part, row = lax.axis_index("dp"), lax.axis_index("rows")
        side, across = row + 1 - 2 * (row % 2), (row + 2) % 4
        corner = across + 1 - 2 * (across % 2)
        mate = part + 1 - 2 * (part % 2)
        mine = part % 2
        barrier = pltpu.get_barrier_semaphore()
        for device in ((part, side), (part, across), (part, corner), (mate, row)):
            pl.semaphore_signal(barrier, inc=1, device_id=device, device_id_type=MESH)
        pl.semaphore_wait(barrier, 4)
        self.pieces = weight_pieces(shards)

        def remote(src, dst, sems, slot, device):
            return pltpu.make_async_remote_copy(
                src_ref=src,
                dst_ref=dst,
                send_sem=sems.at[0, slot],
                recv_sem=sems.at[1, slot],
                device_id=device,
                device_id_type=MESH,
            )

        self.y, self.x, self.own, self.side = [], [], [], []
        for slot, (index, at, rows) in enumerate(self.pieces):
            depth = shards[index].shape[0]
            base = mine * (depth // 2) + at
            start = shards[index].at[pl.ds(pl.multiple_of(base, 64), rows)]
            sent, near, far = (
                fulls[index].at[pl.ds(pl.multiple_of(owner * depth + base, 64), rows)]
                for owner in (row, across, corner)
            )
            self.y.append(
                [
                    remote(start, sent, y_sems, 2 * slot, (part, across)),
                    remote(start, sent, y_sems, 2 * slot + 1, (part, corner)),
                ]
            )
            self.x.append(
                [
                    remote(near, near, x_sems, 2 * slot, (mate, row)),
                    remote(far, far, x_sems, 2 * slot + 1, (mate, row)),
                ]
            )
        for index, shard in enumerate(shards):
            depth = shard.shape[0]
            home = fulls[index].at[pl.ds(pl.multiple_of(row * depth, 64), depth)]
            self.side.append(remote(shard, home, side_sems, index, (part, side)))
            self.own.append(pltpu.make_async_copy(shard, home, own_sem.at[index]))
        for index in range(len(shards)):
            for slot, piece in enumerate(self.pieces):
                if piece[0] == index:
                    self.y[slot][0].start()
                    self.y[slot][1].start()
            self.side[index].start()
            self.own[index].start()

    def forward(self, slot):
        for come, go in zip(self.y[slot], self.x[slot]):
            come.wait_recv()
            go.start()

    def wait_array(self, index):
        for slot, piece in enumerate(self.pieces):
            if piece[0] == index:
                for copy in self.x[slot]:
                    copy.wait_recv()
        self.side[index].wait_recv()
        self.own[index].wait()

    def finish(self):
        for copy in sum(self.y, []) + sum(self.x, []) + self.side:
            copy.wait_send()


def exchange_semaphores(shards):
    total, number = len(weight_pieces(shards)), len(shards)
    return [
        pltpu.SemaphoreType.DMA((number,)),
        pltpu.SemaphoreType.DMA((2, 2 * total)),
        pltpu.SemaphoreType.DMA((2, 2 * total)),
        pltpu.SemaphoreType.DMA((2, number)),
    ]


def dot_rows(left, right):
    return lax.dot_general(left, right, (((1,), (0,)), ((), ())), preferred_element_type=F32)


def dot_turned(left, right):
    return lax.dot_general(left, right, (((1,), (1,)), ((), ())), preferred_element_type=F32)


def make_shift(tall):
    at = lax.broadcasted_iota(jnp.int32, (tall, LANES), 0)
    at = at % HEIGHT
    keeps = {d: (at + d >= 0) & (at + d < HEIGHT) for d in (-3, -2, -1, 1, 2, 3)}

    def shift(value, d):
        return jnp.where(keeps[d], pltpu.roll(value, (-d) % tall, 0), 0.0)

    return shift


def column_sum(value, taps, flip, shift):
    total = value * taps[3]
    for i in (0, 1, 2, 4, 5, 6):
        total = total + shift(value * taps[i], 3 - i if flip else i - 3)
    return total


def square_sum(low, value, high, taps, flip, shift):
    if flip:
        low, high = high, low
    sums = [low * taps[3 * i] + value * taps[3 * i + 1] + high * taps[3 * i + 2] for i in range(3)]
    if flip:
        sums = sums[::-1]
    return sums[1] + shift(sums[0], -1) + shift(sums[2], 1)


def pool_sum(low, value, high, shift):
    total = low + value + high
    return (total + shift(total, -1) + shift(total, 1)) * (1.0 / 9.0)


def lanes(chunk):
    return pl.ds(pl.multiple_of(chunk * LANES, LANES), LANES)


def flat(ref, columns):
    across, tall, _ = ref.shape
    return ref[:, :, columns].reshape(across * tall, columns.size)


def tiles(filters, tile, body):
    @pl.loop(0, filters // tile)
    def _(n):
        body(pl.multiple_of(n * tile, tile))


def planes(first, last, across, body):
    @pl.loop(first, last)
    def _(chunk):
        @pl.loop(0, across)
        def _(w):
            body(w, lanes(chunk))


def tap_rows(ref, columns, number):
    return [ref[pl.ds(i, 1), columns] for i in range(number)]


def clear_ends(rim):
    rim[0] = jnp.zeros(rim.shape[1:], F32)
    rim[rim.shape[0] - 1] = jnp.zeros(rim.shape[1:], F32)


def early_kernel(
    older_hbm,
    newer_hbm,
    grads_hbm,
    square_shard,
    column_shard,
    older_shard,
    newer_shard,
    square_taps,
    column_taps,
    back_a_hbm,
    back_b_hbm,
    cell_hbm,
    older_full_hbm,
    newer_full_hbm,
    older_in,
    newer_in,
    grads_in,
    older_pad,
    newer_pad,
    grads_pad,
    square_full,
    column_full,
    older_full,
    newer_full,
    rim_a,
    rim_b,
    rim_c,
    pre_a,
    pre_b,
    back_a,
    back_b,
    cell_buf,
    in_sems,
    out_sems,
    *exchange_sems,
):
    across, height, channels = older_in.shape
    tall = older_pad.shape[1]
    filters = square_full.shape[0]
    wide = across * tall
    tile = min(filters, 256)
    chunks = filters // LANES
    ins = [
        pltpu.make_async_copy(src, dst, in_sems.at[n])
        for n, (src, dst) in enumerate(
            ((grads_hbm, grads_in), (older_hbm, older_in), (newer_hbm, newer_in))
        )
    ]
    trade = Exchange(
        (square_shard, column_shard, older_shard, newer_shard),
        (square_full, column_full, older_full, newer_full),
        *exchange_sems,
    )
    for copy in ins:
        copy.start()
    outs = []

    def put(src, dst):
        outs.append(pltpu.make_async_copy(src, dst, out_sems.at[len(outs)]))
        outs[-1].start()

    def put_block(q):
        cols = pl.ds(q * filters, filters)
        put(cell_buf.at[:, :, cols], cell_hbm.at[:, :, cols])

    clear_ends(rim_a)
    clear_ends(rim_b)
    shift = make_shift(tall)
    ins[0].wait()
    grads_pad[:, :height, :] = grads_in[...]
    trade.forward(0)
    trade.forward(1)
    ins[1].wait()
    older_pad[:, :height, :] = jnp.maximum(older_in[...], 0)
    ins[2].wait()
    newer_pad[:, :height, :] = jnp.maximum(newer_in[...], 0)
    trade.wait_array(0)
    trade.wait_array(1)

    def back_tile(at):
        cols = pl.ds(at, tile)
        first = dot_turned(flat(grads_pad, pl.ds(0, filters)), square_full[cols, :])
        rim_a[1 : across + 1, :, cols] = first.astype(BF16).astype(F32).reshape(across, tall, tile)
        second = dot_turned(flat(grads_pad, pl.ds(filters, filters)), column_full[cols, :])
        rim_c[:, :, cols] = second.astype(BF16).astype(F32).reshape(across, tall, tile)
        pool_cols = pl.ds(pl.multiple_of(2 * filters + at, tile), tile)
        rim_b[1 : across + 1, :, cols] = grads_pad[:, :, pool_cols].astype(F32)

    tiles(filters, tile, back_tile)

    def back_plane(w, cols):
        taps = tap_rows(square_taps, cols, 9)
        total = square_sum(rim_a[w, :, cols], rim_a[w + 1, :, cols], rim_a[w + 2, :, cols], taps, True, shift)
        same = pl.ds(pl.multiple_of(3 * filters + cols.start, LANES), LANES)
        back_b[w, :, cols] = (total + grads_pad[w, :, same].astype(F32)).astype(BF16)
        total = column_sum(rim_c[w, :, cols], tap_rows(column_taps, cols, 7), True, shift)
        total = total + pool_sum(rim_b[w, :, cols], rim_b[w + 1, :, cols], rim_b[w + 2, :, cols], shift)
        back_a[w, :, cols] = total.astype(BF16)

    older_slots = [n for n, piece in enumerate(trade.pieces) if piece[0] == 2]
    newer_slots = [n for n, piece in enumerate(trade.pieces) if piece[0] == 3]
    done = 0
    for n, slot in enumerate(older_slots):
        until = (n + 1) * chunks // len(older_slots)
        planes(done, until, across, back_plane)
        done = until
        trade.forward(slot)
    put(back_a, back_a_hbm)
    put(back_b, back_b_hbm)
    trade.wait_array(2)
    put(older_full, older_full_hbm)

    def older_tile(at):
        cols = pl.ds(at, tile)
        mixed = dot_rows(older_pad[...].reshape(wide, channels), older_full[:, cols])
        rim_b[1 : across + 1, :, cols] = mixed.astype(BF16).astype(F32).reshape(across, tall, tile)

    tiles(filters, tile, older_tile)

    def older_plane(w, cols):
        total = column_sum(rim_b[w + 1, :, cols], tap_rows(column_taps, cols, 7), False, shift)
        pre_a[w, :, cols] = total.astype(BF16)
        total = pool_sum(rim_b[w, :, cols], rim_b[w + 1, :, cols], rim_b[w + 2, :, cols], shift)
        pool = pl.ds(pl.multiple_of(2 * filters + cols.start, LANES), LANES)
        cell_buf[w, :, pool] = total[:height].astype(BF16)

    done = 0
    for n, slot in enumerate(newer_slots):
        trade.forward(slot)
        until = (n + 1) * chunks // len(newer_slots)
        planes(done, until, across, older_plane)
        done = until
    put_block(2)

    def point_blocks(q, pre, full):
        def point_tile(at):
            term = dot_rows(pre[...].reshape(wide, filters), full[:, pl.ds(at, tile)])
            cols = pl.ds(pl.multiple_of(q * filters + at, tile), tile)
            cell_buf[:, :, cols] = term.reshape(across, tall, tile)[:, :height].astype(BF16)

        tiles(filters, tile, point_tile)
        put_block(q)

    point_blocks(1, pre_a, column_full)
    trade.wait_array(3)
    put(newer_full, newer_full_hbm)

    def newer_tile(at):
        cols = pl.ds(at, tile)
        total = dot_rows(newer_pad[...].reshape(wide, channels), newer_full[:, cols])
        mixed = total.astype(BF16).reshape(across, tall, tile)
        rim_a[1 : across + 1, :, cols] = mixed.astype(F32)
        cell_buf[:, :, pl.ds(pl.multiple_of(3 * filters + at, tile), tile)] = mixed[:, :height]

    tiles(filters, tile, newer_tile)
    put_block(3)

    def newer_plane(w, cols):
        taps = tap_rows(square_taps, cols, 9)
        total = square_sum(rim_a[w, :, cols], rim_a[w + 1, :, cols], rim_a[w + 2, :, cols], taps, False, shift)
        pre_b[w, :, cols] = total.astype(BF16)

    planes(0, chunks, across, newer_plane)
    point_blocks(0, pre_b, square_full)
    trade.finish()
    for copy in outs:
        copy.wait()


def early(older, newer, grads, shards, square_taps, column_taps, count):
    across, height, channels = older.shape
    filters = shards[0].shape[1]
    tall = round_up(height, 16)
    plain = pltpu.VMEM((across, height, channels), BF16)
    padded = pltpu.VMEM((across, tall, channels), BF16)
    rim = pltpu.VMEM((across + 2, tall, filters), F32)
    pre = pltpu.VMEM((across, tall, filters), BF16)
    fulls = [(count * x.shape[0], x.shape[1]) for x in shards]
    anywhere = pl.BlockSpec(memory_space=pl.ANY)
    inside = pl.BlockSpec(memory_space=pltpu.VMEM)
    back = jax.ShapeDtypeStruct((across, tall, filters), BF16)
    return pl.pallas_call(
        early_kernel,
        out_shape=[
            back,
            back,
            jax.ShapeDtypeStruct((across, height, 4 * filters), BF16),
            jax.ShapeDtypeStruct(fulls[2], BF16),
            jax.ShapeDtypeStruct(fulls[3], BF16),
        ],
        in_specs=[anywhere] * 7 + [inside] * 2,
        out_specs=[anywhere] * 5,
        scratch_shapes=[plain] * 3
        + [padded] * 3
        + [pltpu.VMEM(shape, BF16) for shape in fulls]
        + [rim, rim, pltpu.VMEM((across, tall, filters), F32)]
        + [pre] * 4
        + [pltpu.VMEM((across, height, 4 * filters), BF16)]
        + [pltpu.SemaphoreType.DMA((3,)), pltpu.SemaphoreType.DMA((8,))]
        + exchange_semaphores(shards),
        compiler_params=pltpu.CompilerParams(
            collective_id=0, has_side_effects=True, vmem_limit_bytes=60 * 1024 * 1024
        ),
        name="early",
    )(older, newer, grads, *shards, square_taps, column_taps)


def grad_blocks(back, full, pad, buf, hbm, sems, height):
    across, tall, filters = back.shape
    channels = full.shape[0]
    tile = min(filters, 256)
    outs = []
    for q in range(channels // filters):

        def grad_tile(at, base=q * filters):
            cols = pl.ds(pl.multiple_of(base + at, tile), tile)
            term = dot_turned(back[...].reshape(across * tall, filters), full[cols, :])
            keep = pad[:, :, cols] > 0
            term = term.reshape(across, tall, tile)[:, :height]
            buf[:, :, cols] = jnp.where(keep, term, 0.0).astype(BF16)

        tiles(filters, tile, grad_tile)
        cols = pl.ds(q * filters, filters)
        outs.append(pltpu.make_async_copy(buf.at[:, :, cols], hbm.at[:, :, cols], sems.at[q]))
        outs[-1].start()
    return outs


def late_kernel(
    older_hbm,
    newer_hbm,
    back_a_hbm,
    back_b_hbm,
    cell_in_hbm,
    older_full_hbm,
    newer_full_hbm,
    cell_hbm,
    older_out_hbm,
    newer_out_hbm,
    older_in,
    newer_in,
    back_a,
    back_b,
    older_full,
    newer_full,
    older_buf,
    newer_buf,
    in_sems,
    cell_sem,
    older_sems,
    newer_sems,
):
    height = older_in.shape[1]
    loads = [
        pltpu.make_async_copy(src, dst, in_sems.at[n])
        for n, (src, dst) in enumerate(
            (
                (back_a_hbm, back_a),
                (older_full_hbm, older_full),
                (older_hbm, older_in),
                (back_b_hbm, back_b),
                (newer_full_hbm, newer_full),
                (newer_hbm, newer_in),
            )
        )
    ]
    for copy in loads:
        copy.start()
    whole = pltpu.make_async_copy(cell_in_hbm, cell_hbm, cell_sem)
    whole.start()
    for copy in loads[:3]:
        copy.wait()
    outs = grad_blocks(back_a, older_full, older_in, older_buf, older_out_hbm, older_sems, height)
    for copy in loads[3:]:
        copy.wait()
    outs += grad_blocks(back_b, newer_full, newer_in, newer_buf, newer_out_hbm, newer_sems, height)
    for copy in outs + [whole]:
        copy.wait()


def late(older, newer, back_a, back_b, cell, older_full, newer_full):
    plain = pltpu.VMEM(older.shape, BF16)
    back = pltpu.VMEM(back_a.shape, BF16)
    full = pltpu.VMEM(older_full.shape, BF16)
    blocks = older_full.shape[0] // older_full.shape[1]
    anywhere = pl.BlockSpec(memory_space=pl.ANY)
    return pl.pallas_call(
        late_kernel,
        out_shape=[jax.ShapeDtypeStruct(x.shape, BF16) for x in (cell, older, newer)],
        in_specs=[anywhere] * 7,
        out_specs=[anywhere] * 3,
        scratch_shapes=[plain, plain, back, back, full, full, plain, plain]
        + [pltpu.SemaphoreType.DMA((6,)), pltpu.SemaphoreType.DMA(())]
        + [pltpu.SemaphoreType.DMA((blocks,))] * 2,
        compiler_params=pltpu.CompilerParams(vmem_limit_bytes=60 * 1024 * 1024),
        name="late",
    )(older, newer, back_a, back_b, cell, older_full, newer_full)


def whole_images(
    older_output,
    newer_output,
    output_grad,
    older_weight,
    newer_weight,
    square_point,
    column_point,
    square_kernel,
    column_kernel,
):
    count = lax.axis_size("rows")
    older, newer, grads = (jnp.transpose(x, (1, 0, 2)) for x in (older_output, newer_output, output_grad))
    outs = late(
        older,
        newer,
        *early(
            older,
            newer,
            grads,
            (square_point, column_point, older_weight, newer_weight),
            square_kernel.reshape(9, square_point.shape[1]),
            column_kernel,
            count,
        ),
    )
    return tuple(jnp.transpose(x, (1, 0, 2)) for x in outs)


def choose(*arrays):
    height = arrays[0].shape[0]
    routes = lax.axis_size("rows") == 4 and lax.axis_size("dp") % 2 == 0
    if height % HEIGHT == 0 and routes:
        return whole_images(*arrays)
    return local(*arrays)


def solution(mesh):
    in_specs = (
        P(("dp", "rows"), None, None),
        P(("dp", "rows"), None, None),
        P(("dp", "rows"), None, None),
        P("rows", None),
        P("rows", None),
        P("rows", None),
        P("rows", None),
        P(),
        P(),
    )
    out_specs = (
        P(("dp", "rows"), None, None),
        P(("dp", "rows"), None, None),
        P(("dp", "rows"), None, None),
    )
    return jax.shard_map(choose, mesh=mesh, in_specs=in_specs, out_specs=out_specs, check_vma=False)
```

```python
import jax
import jax.numpy as jnp
from jax import lax
from jax.experimental import pallas as pl
from jax.experimental.pallas import tpu as pltpu
from jax.sharding import PartitionSpec as P

MESH = pl.DeviceIdType.MESH
F32 = jnp.float32
BF16 = jnp.bfloat16
LANES = 128

HEIGHT = 30


def with_halo(block, sides, width):
    for axis, dim in sides:
        count = lax.axis_size(axis)
        forward = [(i, i + 1) for i in range(count - 1)]
        backward = [(target, source) for source, target in forward]
        low = lax.ppermute(
            lax.slice_in_dim(block, block.shape[dim] - width, None, axis=dim), axis, forward
        )
        high = lax.ppermute(lax.slice_in_dim(block, 0, width, axis=dim), axis, backward)
        block = jnp.concatenate([low, block, high], axis=dim)
    return block


def same_image(first_row, local_rows, offset):
    row_ids = jnp.arange(local_rows, dtype=jnp.int32) + first_row
    inside = jnp.floor_divide(row_ids + offset, HEIGHT) == jnp.floor_divide(row_ids, HEIGHT)
    return jnp.where(inside, 1.0, 0.0).astype(jnp.float32)[:, None, None]


def square_taps(padded, kernel, flip, first_row):
    full = jnp.pad(padded, ((0, 0), (1, 1), (0, 0))).astype(jnp.float32)
    height = full.shape[0] - 2
    across = full.shape[1] - 2
    total = jnp.zeros((height, across, full.shape[2]), jnp.float32)
    for i in range(3):
        keep = same_image(first_row, height, (2 - i if flip else i) - 1)
        for j in range(3):
            first = 2 - i if flip else i
            second = 2 - j if flip else j
            total = total + full[first : first + height, second : second + across, :] * (
                kernel[i, j] * keep
            )
    return total


def column_taps(padded, kernel, flip, first_row):
    full = padded.astype(jnp.float32)
    height = full.shape[0] - 6
    total = jnp.zeros((height, full.shape[1], full.shape[2]), jnp.float32)
    for i in range(7):
        first = 6 - i if flip else i
        keep = same_image(first_row, height, first - 3)
        total = total + full[first : first + height, :, :] * (kernel[i] * keep)
    return total


def local(
    older_output,
    newer_output,
    output_grad,
    older_weight,
    newer_weight,
    square_point,
    column_point,
    square_kernel,
    column_kernel,
):
    height, across, channels = older_output.shape
    filters = square_point.shape[1]
    shape_three = (height, across, filters)
    first_row = lax.axis_index("rows") * height
    pool_kernel = jnp.full((3, 3, filters), 1.0 / 9.0, jnp.float32)
    older_flat = older_output.reshape(-1, channels)
    newer_flat = newer_output.reshape(-1, channels)
    older_relu = jnp.maximum(older_flat, 0)
    newer_relu = jnp.maximum(newer_flat, 0)
    older_full, newer_full = (
        lax.all_gather(older_weight, "rows", axis=0, tiled=True),
        lax.all_gather(newer_weight, "rows", axis=0, tiled=True),
    )
    older_sum = jnp.dot(older_relu, older_full, preferred_element_type=jnp.float32)
    newer_sum = jnp.dot(newer_relu, newer_full, preferred_element_type=jnp.float32)
    older_mixed = older_sum.astype(jnp.bfloat16).reshape(shape_three)
    newer_mixed = newer_sum.astype(jnp.bfloat16).reshape(shape_three)
    square_full, column_full = (
        lax.all_gather(square_point, "rows", axis=0, tiled=True),
        lax.all_gather(column_point, "rows", axis=0, tiled=True),
    )
    older_rim = with_halo(older_mixed, (("rows", 0),), 3)
    newer_rim = with_halo(newer_mixed, (("rows", 0),), 1)
    square_pre = (
        square_taps(newer_rim, square_kernel, False, first_row)
        .astype(jnp.bfloat16)
        .reshape(-1, filters)
    )
    column_pre = (
        column_taps(older_rim, column_kernel, False, first_row)
        .astype(jnp.bfloat16)
        .reshape(-1, filters)
    )
    pooled = square_taps(older_rim[2:-2], pool_kernel, False, first_row).reshape(-1, filters)
    square_branch = jnp.dot(square_pre, square_full, preferred_element_type=jnp.float32)
    column_branch = jnp.dot(column_pre, column_full, preferred_element_type=jnp.float32)
    cell_output = jnp.concatenate(
        [
            square_branch,
            column_branch,
            pooled,
            newer_mixed.reshape(-1, filters).astype(jnp.float32),
        ],
        axis=1,
    )
    cell_output = cell_output.astype(jnp.bfloat16).reshape(height, across, 4 * filters)
    grads = output_grad.reshape(-1, 4 * filters)
    grad_square = grads[:, :filters]
    grad_column = grads[:, filters : 2 * filters]
    grad_pool = grads[:, 2 * filters : 3 * filters].reshape(shape_three)
    grad_same = grads[:, 3 * filters :].reshape(shape_three)
    square_back = (
        jnp.dot(grad_square, square_full.T, preferred_element_type=jnp.float32)
        .astype(jnp.bfloat16)
        .reshape(shape_three)
    )
    column_back = (
        jnp.dot(grad_column, column_full.T, preferred_element_type=jnp.float32)
        .astype(jnp.bfloat16)
        .reshape(shape_three)
    )
    column_rim = with_halo(column_back, (("rows", 0),), 3)
    square_rim, pool_rim = (
        with_halo(square_back, (("rows", 0),), 1),
        with_halo(grad_pool, (("rows", 0),), 1),
    )
    newer_back = (
        (square_taps(square_rim, square_kernel, True, first_row) + grad_same.astype(jnp.float32))
        .astype(jnp.bfloat16)
        .reshape(-1, filters)
    )
    older_back = (
        (
            column_taps(column_rim, column_kernel, True, first_row)
            + square_taps(pool_rim, pool_kernel, True, first_row)
        )
        .astype(jnp.bfloat16)
        .reshape(-1, filters)
    )
    older_mask = jnp.where(older_flat > 0, 1.0, 0.0).astype(jnp.float32)
    newer_mask = jnp.where(newer_flat > 0, 1.0, 0.0).astype(jnp.float32)
    older_term = jnp.dot(older_back, older_full.T, preferred_element_type=jnp.float32)
    newer_term = jnp.dot(newer_back, newer_full.T, preferred_element_type=jnp.float32)
    older_grad = (older_term * older_mask).astype(jnp.bfloat16).reshape(older_output.shape)
    newer_grad = (newer_term * newer_mask).astype(jnp.bfloat16).reshape(newer_output.shape)
    return (cell_output, older_grad, newer_grad)


def round_up(value, step):
    return -(-value // step) * step


def weight_pieces(shards):
    pieces = []
    for index, shard in enumerate(shards):
        half = shard.shape[0] // 2
        rows = min(half, 128)
        pieces += [(index, at, rows) for at in range(0, half, rows)]
    return pieces


class Exchange:
    def __init__(self, shards, fulls, own_sem, y_sems, x_sems, side_sems, pass_sems):
        self.own = []
        for index, shard in enumerate(shards):
            depth = shard.shape[0]
            home = pl.ds(pl.multiple_of(lax.axis_index("rows") * depth, 64), depth)
            self.own.append(pltpu.make_async_copy(shard, fulls[index].at[home], own_sem.at[index]))
            self.own[index].start()
        part, row = lax.axis_index("dp"), lax.axis_index("rows")
        side, across = row + 1 - 2 * (row % 2), (row + 2) % 4
        mate = part + 1 - 2 * (part % 2)
        mine, theirs = part % 2, 1 - part % 2
        barrier = pltpu.get_barrier_semaphore()
        for device in ((part, side), (part, across), (mate, row)):
            pl.semaphore_signal(barrier, inc=1, device_id=device, device_id_type=MESH)
        pl.semaphore_wait(barrier, 3)
        self.pieces = weight_pieces(shards)

        def span(index, owner, half, at, rows):
            depth = shards[index].shape[0]
            return pl.ds(pl.multiple_of(owner * depth + half * (depth // 2) + at, 64), rows)

        def remote(src, dst, sems, slot, device):
            return pltpu.make_async_remote_copy(
                src_ref=src,
                dst_ref=dst,
                send_sem=sems.at[0, slot],
                recv_sem=sems.at[1, slot],
                device_id=device,
                device_id_type=MESH,
            )

        self.y, self.x, self.low, self.high, self.side = [], [], [], [], []
        total = len(self.pieces)
        for slot, (index, at, rows) in enumerate(self.pieces):
            sent = fulls[index].at[span(index, row, mine, at, rows)]
            got = fulls[index].at[span(index, across, mine, at, rows)]
            other = fulls[index].at[span(index, across, theirs, at, rows)]
            self.y.append(remote(sent, sent, y_sems, slot, (part, across)))
            self.x.append(remote(got, got, x_sems, slot, (mate, row)))
            self.low.append(remote(got, got, pass_sems, slot, (part, side)))
            self.high.append(remote(other, other, pass_sems, total + slot, (part, side)))
        for index, shard in enumerate(shards):
            depth = shard.shape[0]
            home = fulls[index].at[pl.ds(pl.multiple_of(row * depth, 64), depth)]
            self.side.append(remote(home, home, side_sems, index, (part, side)))
        for index in range(len(shards)):
            self.own[index].wait()
            for slot, piece in enumerate(self.pieces):
                if piece[0] == index:
                    self.y[slot].start()

    def forward(self, slot):
        if slot < len(self.pieces):
            self.y[slot].wait_recv()
            self.x[slot].start()
            self.low[slot].start()
        if slot > 0:
            self.x[slot - 1].wait_recv()
            self.high[slot - 1].start()

    def wait_array(self, index):
        for slot, piece in enumerate(self.pieces):
            if piece[0] == index:
                self.low[slot].wait_recv()
                self.high[slot].wait_recv()
        self.side[index].wait_recv()

    def finish(self):
        for copy in self.y + self.x + self.low + self.high + self.side:
            copy.wait_send()


def exchange_semaphores(shards):
    total, number = len(weight_pieces(shards)), len(shards)
    return [
        pltpu.SemaphoreType.DMA((number,)),
        pltpu.SemaphoreType.DMA((2, total)),
        pltpu.SemaphoreType.DMA((2, total)),
        pltpu.SemaphoreType.DMA((2, number)),
        pltpu.SemaphoreType.DMA((2, 2 * total)),
    ]


def dot_rows(left, right):
    return lax.dot_general(left, right, (((1,), (0,)), ((), ())), preferred_element_type=F32)


def dot_turned(left, right):
    return lax.dot_general(left, right, (((1,), (1,)), ((), ())), preferred_element_type=F32)


def make_shift(tall):
    at = lax.broadcasted_iota(jnp.int32, (tall, LANES), 0)
    at = at % HEIGHT
    keeps = {d: (at + d >= 0) & (at + d < HEIGHT) for d in (-3, -2, -1, 1, 2, 3)}

    def shift(value, d):
        return jnp.where(keeps[d], pltpu.roll(value, (-d) % tall, 0), 0.0)

    return shift


def column_sum(value, taps, flip, shift):
    total = value * taps[3]
    for i in (0, 1, 2, 4, 5, 6):
        total = total + shift(value * taps[i], 3 - i if flip else i - 3)
    return total


def square_sum(low, value, high, taps, flip, shift):
    if flip:
        low, high = high, low
    sums = [low * taps[3 * i] + value * taps[3 * i + 1] + high * taps[3 * i + 2] for i in range(3)]
    if flip:
        sums = sums[::-1]
    return sums[1] + shift(sums[0], -1) + shift(sums[2], 1)


def pool_sum(low, value, high, shift):
    total = low + value + high
    return (total + shift(total, -1) + shift(total, 1)) * (1.0 / 9.0)


def lanes(chunk):
    return pl.ds(pl.multiple_of(chunk * LANES, LANES), LANES)


def flat(ref, columns):
    across, tall, _ = ref.shape
    return ref[:, :, columns].reshape(across * tall, columns.size)


def tiles(filters, tile, body):
    @pl.loop(0, filters // tile)
    def _(n):
        body(pl.multiple_of(n * tile, tile))


def planes(first, last, across, body):
    @pl.loop(first, last)
    def _(chunk):
        @pl.loop(0, across)
        def _(w):
            body(w, lanes(chunk))


def tap_rows(ref, columns, number):
    return [ref[pl.ds(i, 1), columns] for i in range(number)]


def clear_ends(rim):
    rim[0] = jnp.zeros(rim.shape[1:], F32)
    rim[rim.shape[0] - 1] = jnp.zeros(rim.shape[1:], F32)


def early_kernel(
    older_hbm,
    newer_hbm,
    grads_hbm,
    square_shard,
    column_shard,
    older_shard,
    newer_shard,
    square_taps,
    column_taps,
    back_a_hbm,
    back_b_hbm,
    cell_hbm,
    older_full_hbm,
    newer_full_hbm,
    older_in,
    newer_in,
    grads_in,
    older_pad,
    newer_pad,
    grads_pad,
    square_full,
    column_full,
    older_full,
    newer_full,
    rim_a,
    rim_b,
    rim_c,
    pre_a,
    pre_b,
    back_a,
    back_b,
    cell_buf,
    in_sems,
    out_sems,
    *exchange_sems,
):
    across, height, channels = older_in.shape
    tall = older_pad.shape[1]
    filters = square_full.shape[0]
    wide = across * tall
    tile = min(filters, 256)
    chunks = filters // LANES
    ins = [
        pltpu.make_async_copy(src, dst, in_sems.at[n])
        for n, (src, dst) in enumerate(
            ((grads_hbm, grads_in), (older_hbm, older_in), (newer_hbm, newer_in))
        )
    ]
    trade = Exchange(
        (square_shard, column_shard, older_shard, newer_shard),
        (square_full, column_full, older_full, newer_full),
        *exchange_sems,
    )
    for copy in ins:
        copy.start()
    outs = []

    def put(src, dst):
        outs.append(pltpu.make_async_copy(src, dst, out_sems.at[len(outs)]))
        outs[-1].start()

    def put_block(q):
        cols = pl.ds(q * filters, filters)
        put(cell_buf.at[:, :, cols], cell_hbm.at[:, :, cols])

    for index in range(3):
        trade.side[index].start()
    clear_ends(rim_a)
    clear_ends(rim_b)
    shift = make_shift(tall)
    ins[0].wait()
    grads_pad[:, :height, :] = grads_in[...]
    slots = [[n for n, piece in enumerate(trade.pieces) if piece[0] == index] for index in range(4)]
    for slot in slots[0] + slots[1]:
        trade.forward(slot)
    ins[1].wait()
    older_pad[:, :height, :] = jnp.maximum(older_in[...], 0)
    ins[2].wait()
    newer_pad[:, :height, :] = jnp.maximum(newer_in[...], 0)
    trade.forward(slots[2][0])
    trade.wait_array(0)
    trade.wait_array(1)

    def back_tile(at):
        cols = pl.ds(at, tile)
        first = dot_turned(flat(grads_pad, pl.ds(0, filters)), square_full[cols, :])
        rim_a[1 : across + 1, :, cols] = first.astype(BF16).astype(F32).reshape(across, tall, tile)
        second = dot_turned(flat(grads_pad, pl.ds(filters, filters)), column_full[cols, :])
        rim_c[:, :, cols] = second.astype(BF16).astype(F32).reshape(across, tall, tile)
        pool_cols = pl.ds(pl.multiple_of(2 * filters + at, tile), tile)
        rim_b[1 : across + 1, :, cols] = grads_pad[:, :, pool_cols].astype(F32)

    tiles(filters, tile, back_tile)

    def back_plane(w, cols):
        taps = tap_rows(square_taps, cols, 9)
        total = square_sum(rim_a[w, :, cols], rim_a[w + 1, :, cols], rim_a[w + 2, :, cols], taps, True, shift)
        same = pl.ds(pl.multiple_of(3 * filters + cols.start, LANES), LANES)
        back_b[w, :, cols] = (total + grads_pad[w, :, same].astype(F32)).astype(BF16)
        total = column_sum(rim_c[w, :, cols], tap_rows(column_taps, cols, 7), True, shift)
        total = total + pool_sum(rim_b[w, :, cols], rim_b[w + 1, :, cols], rim_b[w + 2, :, cols], shift)
        back_a[w, :, cols] = total.astype(BF16)

    done = 0
    for n, slot in enumerate(slots[2]):
        until = (n + 1) * chunks // len(slots[2])
        planes(done, until, across, back_plane)
        done = until
        trade.forward(slot + 1)
    trade.side[3].start()
    put(back_a, back_a_hbm)
    put(back_b, back_b_hbm)
    trade.wait_array(2)
    put(older_full, older_full_hbm)

    def older_tile(at):
        cols = pl.ds(at, tile)
        mixed = dot_rows(older_pad[...].reshape(wide, channels), older_full[:, cols])
        rim_b[1 : across + 1, :, cols] = mixed.astype(BF16).astype(F32).reshape(across, tall, tile)

    tiles(filters, tile, older_tile)

    def older_plane(w, cols):
        total = column_sum(rim_b[w + 1, :, cols], tap_rows(column_taps, cols, 7), False, shift)
        pre_a[w, :, cols] = total.astype(BF16)
        total = pool_sum(rim_b[w, :, cols], rim_b[w + 1, :, cols], rim_b[w + 2, :, cols], shift)
        pool = pl.ds(pl.multiple_of(2 * filters + cols.start, LANES), LANES)
        cell_buf[w, :, pool] = total[:height].astype(BF16)

    done = 0
    for n, slot in enumerate(slots[3]):
        trade.forward(slot + 1)
        until = (n + 1) * chunks // len(slots[3])
        planes(done, until, across, older_plane)
        done = until
    put_block(2)

    def point_blocks(q, pre, full):
        def point_tile(at):
            term = dot_rows(pre[...].reshape(wide, filters), full[:, pl.ds(at, tile)])
            cols = pl.ds(pl.multiple_of(q * filters + at, tile), tile)
            cell_buf[:, :, cols] = term.reshape(across, tall, tile)[:, :height].astype(BF16)

        tiles(filters, tile, point_tile)
        put_block(q)

    point_blocks(1, pre_a, column_full)
    trade.wait_array(3)
    put(newer_full, newer_full_hbm)

    def newer_tile(at):
        cols = pl.ds(at, tile)
        total = dot_rows(newer_pad[...].reshape(wide, channels), newer_full[:, cols])
        mixed = total.astype(BF16).reshape(across, tall, tile)
        rim_a[1 : across + 1, :, cols] = mixed.astype(F32)
        cell_buf[:, :, pl.ds(pl.multiple_of(3 * filters + at, tile), tile)] = mixed[:, :height]

    tiles(filters, tile, newer_tile)
    put_block(3)

    def newer_plane(w, cols):
        taps = tap_rows(square_taps, cols, 9)
        total = square_sum(rim_a[w, :, cols], rim_a[w + 1, :, cols], rim_a[w + 2, :, cols], taps, False, shift)
        pre_b[w, :, cols] = total.astype(BF16)

    planes(0, chunks, across, newer_plane)
    point_blocks(0, pre_b, square_full)
    trade.finish()
    for copy in outs:
        copy.wait()


def early(older, newer, grads, shards, square_taps, column_taps, count):
    across, height, channels = older.shape
    filters = shards[0].shape[1]
    tall = round_up(height, 16)
    plain = pltpu.VMEM((across, height, channels), BF16)
    padded = pltpu.VMEM((across, tall, channels), BF16)
    rim = pltpu.VMEM((across + 2, tall, filters), F32)
    pre = pltpu.VMEM((across, tall, filters), BF16)
    fulls = [(count * x.shape[0], x.shape[1]) for x in shards]
    anywhere = pl.BlockSpec(memory_space=pl.ANY)
    inside = pl.BlockSpec(memory_space=pltpu.VMEM)
    back = jax.ShapeDtypeStruct((across, tall, filters), BF16)
    return pl.pallas_call(
        early_kernel,
        out_shape=[
            back,
            back,
            jax.ShapeDtypeStruct((across, height, 4 * filters), BF16),
            jax.ShapeDtypeStruct(fulls[2], BF16),
            jax.ShapeDtypeStruct(fulls[3], BF16),
        ],
        in_specs=[anywhere] * 7 + [inside] * 2,
        out_specs=[anywhere] * 5,
        scratch_shapes=[plain] * 3
        + [padded] * 3
        + [pltpu.VMEM(shape, BF16) for shape in fulls]
        + [rim, rim, pltpu.VMEM((across, tall, filters), F32)]
        + [pre] * 4
        + [pltpu.VMEM((across, height, 4 * filters), BF16)]
        + [pltpu.SemaphoreType.DMA((3,)), pltpu.SemaphoreType.DMA((8,))]
        + exchange_semaphores(shards),
        compiler_params=pltpu.CompilerParams(
            collective_id=0, has_side_effects=True, vmem_limit_bytes=60 * 1024 * 1024
        ),
        name="early",
    )(older, newer, grads, *shards, square_taps, column_taps)


def grad_blocks(back, full, pad, buf, hbm, sems, height):
    across, tall, filters = back.shape
    channels = full.shape[0]
    tile = min(filters, 256)
    outs = []
    for q in range(channels // filters):

        def grad_tile(at, base=q * filters):
            cols = pl.ds(pl.multiple_of(base + at, tile), tile)
            term = dot_turned(back[...].reshape(across * tall, filters), full[cols, :])
            keep = pad[:, :, cols] > 0
            term = term.reshape(across, tall, tile)[:, :height]
            buf[:, :, cols] = jnp.where(keep, term, 0.0).astype(BF16)

        tiles(filters, tile, grad_tile)
        cols = pl.ds(q * filters, filters)
        outs.append(pltpu.make_async_copy(buf.at[:, :, cols], hbm.at[:, :, cols], sems.at[q]))
        outs[-1].start()
    return outs


def late_kernel(
    older_hbm,
    newer_hbm,
    back_a_hbm,
    back_b_hbm,
    cell_in_hbm,
    older_full_hbm,
    newer_full_hbm,
    cell_hbm,
    older_out_hbm,
    newer_out_hbm,
    older_in,
    newer_in,
    back_a,
    back_b,
    older_full,
    newer_full,
    older_buf,
    newer_buf,
    cell_buf,
    in_sems,
    cell_sem,
    older_sems,
    newer_sems,
):
    height = older_in.shape[1]
    loads = [
        pltpu.make_async_copy(src, dst, in_sems.at[n])
        for n, (src, dst) in enumerate(
            (
                (back_a_hbm, back_a),
                (older_full_hbm, older_full),
                (older_hbm, older_in),
                (back_b_hbm, back_b),
                (newer_full_hbm, newer_full),
                (newer_hbm, newer_in),
                (cell_in_hbm, cell_buf),
            )
        )
    ]
    for copy in loads:
        copy.start()
    for copy in loads[:3]:
        copy.wait()
    outs = grad_blocks(back_a, older_full, older_in, older_buf, older_out_hbm, older_sems, height)
    for copy in loads[3:]:
        copy.wait()
    whole = pltpu.make_async_copy(cell_buf, cell_hbm, cell_sem)
    whole.start()
    outs += grad_blocks(back_b, newer_full, newer_in, newer_buf, newer_out_hbm, newer_sems, height)
    for copy in outs + [whole]:
        copy.wait()


def late(older, newer, back_a, back_b, cell, older_full, newer_full):
    plain = pltpu.VMEM(older.shape, BF16)
    back = pltpu.VMEM(back_a.shape, BF16)
    full = pltpu.VMEM(older_full.shape, BF16)
    blocks = older_full.shape[0] // older_full.shape[1]
    anywhere = pl.BlockSpec(memory_space=pl.ANY)
    return pl.pallas_call(
        late_kernel,
        out_shape=[jax.ShapeDtypeStruct(x.shape, BF16) for x in (cell, older, newer)],
        in_specs=[anywhere] * 7,
        out_specs=[anywhere] * 3,
        scratch_shapes=[plain, plain, back, back, full, full, plain, plain, plain]
        + [pltpu.SemaphoreType.DMA((7,)), pltpu.SemaphoreType.DMA(())]
        + [pltpu.SemaphoreType.DMA((blocks,))] * 2,
        compiler_params=pltpu.CompilerParams(vmem_limit_bytes=60 * 1024 * 1024),
        name="late",
    )(older, newer, back_a, back_b, cell, older_full, newer_full)


def whole_images(
    older_output,
    newer_output,
    output_grad,
    older_weight,
    newer_weight,
    square_point,
    column_point,
    square_kernel,
    column_kernel,
):
    count = lax.axis_size("rows")
    older, newer, grads = (jnp.transpose(x, (1, 0, 2)) for x in (older_output, newer_output, output_grad))
    outs = late(
        older,
        newer,
        *early(
            older,
            newer,
            grads,
            (square_point, column_point, older_weight, newer_weight),
            square_kernel.reshape(9, square_point.shape[1]),
            column_kernel,
            count,
        ),
    )
    return tuple(jnp.transpose(x, (1, 0, 2)) for x in outs)


def choose(*arrays):
    height = arrays[0].shape[0]
    routes = lax.axis_size("rows") == 4 and lax.axis_size("dp") % 2 == 0
    if height % HEIGHT == 0 and routes:
        return whole_images(*arrays)
    return local(*arrays)


def solution(mesh):
    in_specs = (
        P(("dp", "rows"), None, None),
        P(("dp", "rows"), None, None),
        P(("dp", "rows"), None, None),
        P("rows", None),
        P("rows", None),
        P("rows", None),
        P("rows", None),
        P(),
        P(),
    )
    out_specs = (
        P(("dp", "rows"), None, None),
        P(("dp", "rows"), None, None),
        P(("dp", "rows"), None, None),
    )
    return jax.shard_map(choose, mesh=mesh, in_specs=in_specs, out_specs=out_specs, check_vma=False)
```
